256 devices in a mesh: row: 16 (over x_lo, y, core), col: 16 (over z, x_hi).
Axes of the slice: x: 4 (x_hi: 2, x_lo: 2; x = x_hi * 2 + x_lo), y: 4, z: 8, core: 2. Of those that a mesh axis runs over, the one named last changes fastest.
Arguments:
- tokens: bfloat16 [6144, 16384], P('row', 'col'), may hold values from -6 to 6
- gate_weight: bfloat16 [16384, 26624], P('row', 'col'), may hold values from -0.046875 to 0.046875
Outputs:
- gate_partial: float32 [6144, 26624], P('row', 'col')
The draws below stay inside these ranges and needn't reach their ends.
All inputs are finite; a program needn't handle non-finite values.
Results may differ from the reference program's by a relative error of at most 0.0003.
Values may be sent and summed in bfloat16 or wider, within the bound.
No kernel may reach another device: no remote copies, remote signals or barrier semaphores. Data moves between devices by JAX's collectives and lax.ppermute only.
A program may use at most 64 MiB of HBM per device.

```python
import jax
import jax.numpy as jnp
from jax import lax

D = 16384
FF = 26624
TOK_DEV = 384
STEPS = 4
TOKENS = 6144
N_ROW = 16
N_COL = 16


def levels(stream_key, dims, split, least, high):
    factor_of, own = 1.0, jax.random.fold_in(stream_key, 6)
    for position, blocks in split:
        steps = jnp.exp(jax.random.uniform(jax.random.fold_in(own, position), (blocks,), jnp.float32, least / len(split), high / len(split)))
        factor_of = factor_of * jnp.repeat(steps, dims[position] // blocks).reshape([-1 if axis == position else 1 for axis in range(len(dims))])
    return factor_of


def noise(key, shape, width, most, shards=(), kind=jnp.bfloat16):
    gain = levels(key, shape, shards, -0.22, 0.18) if shards else 1.0
    drawn = jax.random.normal(key, shape, jnp.float32) * width * gain
    return jnp.minimum(jnp.maximum(drawn, -most), most).astype(kind)


def setup_inputs(seed: int = 0) -> dict:
    seeds = jax.random.split(jax.random.key(seed), 3)
    return {
        "tokens": noise(seeds[0], (TOKENS, D), 1.0, 6.0, ((0, 16), (1, 16))),
        "gate_weight": noise(seeds[1], (D, FF), D ** -0.5, 0.046875, ((0, 16), (1, 16))),
    }


def reference(tokens, gate_weight):
    block_rows = D // N_ROW
    hidden_cols = FF // N_COL
    ratio = N_ROW // N_COL
    grouped = tokens.reshape(N_ROW, TOK_DEV, N_ROW, block_rows)
    weights = gate_weight.reshape(N_ROW, block_rows, N_COL, hidden_cols)
    columns = jnp.arange(N_COL, dtype=jnp.int32)

    def one_block(inputs):
        token_block, row_index = inputs
        running = jnp.zeros((TOK_DEV, N_COL, hidden_cols), jnp.float32)
        for advance in range(STEPS):
            width_index = ((row_index + ratio * columns + advance) % N_ROW).astype(jnp.int32)
            chosen = jnp.take(token_block, width_index, axis=1).astype(jnp.float32)
            selected = weights[width_index, :, columns, :].astype(jnp.float32)
            running = running + jnp.einsum("tjd,jdf->tjf", chosen, selected)
        return running

    result = lax.map(one_block, (grouped, jnp.arange(N_ROW, dtype=jnp.int32)))
    return result.reshape(TOKENS, FF)
```

```python
import functools

import jax
import jax.numpy as jnp
import numpy as np
from jax import lax
from jax.experimental import pallas as pl
from jax.experimental.pallas import tpu as pltpu
from jax.sharding import PartitionSpec as P

XS, YS, ZS = 2, 4, 8
BOTH = ("row", "col")
PARTS = 2

ROUTES = {
    (0, 0, 3): (
        (((0, 3, 7, 6),), ((1, 1, 6, 7),)),
        (((2, 0), (1, 6, 7)), ((0, 0, 3, 7),)),
        (((1, 0), (0, 1)), ((2, 0), (0, 1))),
        (((0, 0, 1), (2, 2)), ((1, 0, 1, 2),)),
    ),
    (0, 0, 2): (
        (((2, 7),), ((2, 7),)),
        (((2, 0),), ((2, 0),)),
        (((2, 1),), ((2, 1),)),
        (((2, 2),), ((2, 2),)),
    ),
    (0, 1, 3): (
        (((1, 7, 6),), ((0, 1, 6), (2, 7))),
        (((1, 0, 3, 7),), ((1, 6, 7, 0),)),
        (((0, 0), (1, 1)), ((1, 1, 0),)),
        (((0, 2, 1),), ((1, 0, 1), (2, 2))),
    ),
    (0, 1, 2): (
        (((1, 2, 6, 7),), ((1, 3, 7, 6),)),
        (((2, 0), (0, 6, 7)), ((0, 0, 7),)),
        (((1, 1, 0),), ((1, 0, 1),)),
        (((1, 0, 1, 2),), ((0, 2, 1),)),
    ),
    (1, 0, 3): (
        (((0, 1, 5, 6), (1, 7)), ((0, 5, 6, 7),)),
        (((2, 0), (1, 6, 7)), ((1, 6, 7, 0),)),
        (((1, 1), (0, 7, 0)), ((0, 7, 0, 1),)),
        (((1, 0, 1), (0, 2)), ((0, 0, 1, 2),)),
    ),
    (1, 0, 2): (
        (((0, 7, 6),), ((0, 7, 6),)),
        (((0, 0, 7),), ((1, 0, 3, 7),)),
        (((0, 1, 0),), ((1, 1, 0),)),
        (((1, 2, 1),), ((0, 2, 1),)),
    ),
    (1, 1, 3): (
        (((0, 7, 6, 5),), ((0, 7, 6, 5),)),
        (((1, 0, 7, 6),), ((0, 0, 3, 7), (2, 6))),
        (((0, 1, 0, 7),), ((0, 1, 0), (1, 6, 7))),
        (((0, 0, 1), (2, 2)), ((0, 2, 1, 0),)),
    ),
    (1, 1, 2): (
        (((1, 1, 5, 6),), ((0, 1, 5, 6),)),
        (((0, 6, 7),), ((0, 2, 6, 7),)),
        (((1, 7, 0),), ((0, 7, 0),)),
        (((0, 0, 1),), ((1, 0, 1),)),
    ),
    (2, 0, 3): (
        (((1, 4, 5, 6),), ((0, 4, 5, 6),)),
        (((0, 5, 6, 7),), ((1, 5, 7, 6),)),
        (((1, 1, 0), (0, 6, 7)), ((0, 6), (1, 7, 0))),
        (((0, 0), (2, 1), (1, 7)), ((1, 0, 1), (0, 7))),
    ),
    (2, 0, 2): (
        (((0, 1, 5, 6),), ((0, 3, 6, 5),)),
        (((0, 2, 6, 7),), ((1, 7, 6),)),
        (((0, 0, 7),), ((1, 1, 0, 7),)),
        (((1, 0, 1),), ((0, 1, 0),)),
    ),
    (2, 1, 3): (
        (((0, 4, 5, 6),), ((1, 4, 5, 6),)),
        (((1, 7, 6, 5),), ((1, 5, 6, 7),)),
        (((0, 1, 0), (1, 6, 7)), ((0, 1, 0), (1, 6, 7))),
        (((1, 0), (2, 1), (0, 7)), ((0, 0), (2, 1), (1, 7))),
    ),
    (2, 1, 2): (
        (((1, 4, 5),), ((0, 4, 5),)),
        (((0, 5, 6),), ((1, 5, 6),)),
        (((1, 6, 7),), ((1, 6, 7),)),
        (((0, 0), (2, 7)), ((1, 0), (2, 7))),
    ),
    (3, 0, 3): (
        (((1, 4, 5), (2, 3)), ((0, 4, 5), (1, 3))),
        (((0, 6, 5, 4),), ((1, 6, 5, 4),)),
        (((1, 7, 6, 5),), ((0, 6, 7, 5),)),
        (((2, 0), (0, 7, 6)), ((1, 0), (0, 7, 6))),
    ),
    (3, 0, 2): (
        (((0, 4, 5),), ((0, 4, 5),)),
        (((1, 5, 6),), ((1, 5, 6),)),
        (((1, 6, 7),), ((1, 6, 7),)),
        (((2, 0), (1, 7)), ((2, 0), (1, 7))),
    ),
    (3, 1, 3): (
        (((1, 4, 5), (0, 3)), ((1, 4, 5), (2, 3))),
        (((1, 5, 4, 6),), ((0, 5, 4, 6),)),
        (((0, 5, 6, 7),), ((1, 5, 6, 7),)),
        (((0, 0), (1, 7, 6)), ((2, 0), (0, 7, 6))),
    ),
    (3, 1, 2): (
        (((1, 4), (2, 3)), ((1, 4), (0, 3))),
        (((1, 5, 4),), ((0, 5, 4),)),
        (((1, 6, 5),), ((1, 6, 5),)),
        (((0, 7, 6),), ((1, 7, 6),)),
    ),
    (4, 0, 3): (
        (((0, 4), (2, 2), (1, 3)), ((0, 4), (2, 2), (1, 3))),
        (((1, 4, 5), (0, 2, 3)), ((1, 5, 4), (0, 2, 3))),
        (((1, 6, 4, 5),), ((1, 6, 5, 4),)),
        (((0, 7, 6, 5),), ((0, 7, 6, 5),)),
    ),
    (4, 0, 2): (
        (((0, 4), (2, 3)), ((2, 4), (0, 3))),
        (((0, 5, 4),), ((0, 5, 4),)),
        (((1, 6, 5),), ((1, 6, 5),)),
        (((1, 7, 6),), ((1, 7, 6),)),
    ),
    (4, 1, 3): (
        (((0, 4), (1, 3, 2)), ((2, 4), (0, 3, 2))),
        (((1, 4, 3), (0, 5)), ((1, 5, 4), (0, 2, 3))),
        (((1, 6, 4, 5),), ((1, 6, 5, 4),)),
        (((0, 7, 6, 5),), ((1, 7, 6, 5),)),
    ),
    (4, 1, 2): (
        (((2, 2), (0, 3)), ((0, 2, 3),)),
        (((1, 2, 3, 4),), ((0, 3, 4),)),
        (((0, 4, 5),), ((0, 1, 5, 4),)),
        (((1, 0, 5, 6),), ((1, 2, 6, 5),)),
    ),
    (5, 0, 3): (
        (((1, 1, 2, 3),), ((1, 1), (0, 3, 2))),
        (((0, 2, 3, 4),), ((2, 4), (1, 2, 3))),
        (((1, 3, 4, 5),), ((2, 5), (1, 3, 0, 4))),
        (((1, 4, 5, 6),), ((1, 4, 5, 6),)),
    ),
    (5, 0, 2): (
        (((1, 3, 2),), ((0, 3, 2),)),
        (((1, 4, 3),), ((1, 4, 3),)),
        (((1, 5, 4),), ((1, 1, 5, 4),)),
        (((0, 2, 6, 5),), ((1, 2, 6, 5),)),
    ),
    (5, 1, 3): (
        (((2, 1), (1, 3, 2)), ((1, 3, 2, 1),)),
        (((0, 4, 3, 2),), ((0, 4, 3), (2, 2))),
        (((0, 5, 4, 3),), ((0, 5, 4), (2, 3))),
        (((1, 6, 5, 4),), ((2, 4), (0, 2, 6, 5))),
    ),
    (5, 1, 2): (
        (((1, 1, 2),), ((1, 1, 2),)),
        (((1, 2, 3),), ((1, 2, 3),)),
        (((0, 3, 4),), ((0, 3, 0, 4),)),
        (((1, 4, 5),), ((1, 4, 5),)),
    ),
    (6, 0, 3): (
        (((0, 1, 2),), ((0, 3, 2, 1),)),
        (((0, 2, 3),), ((1, 2, 3),)),
        (((0, 3, 4),), ((1, 3, 4),)),
        (((1, 2, 5, 4),), ((0, 2, 5, 4),)),
    ),
    (6, 0, 2): (
        (((2, 1), (0, 3, 2)), ((1, 1, 2),)),
        (((1, 2), (2, 3)), ((0, 3, 2),)),
        (((0, 1, 4, 3),), ((1, 3, 4),)),
        (((1, 0, 4, 5),), ((0, 0, 4, 5),)),
    ),
    (6, 1, 3): (
        (((0, 1), (1, 3, 2)), ((2, 1), (1, 3, 2))),
        (((0, 2), (2, 3)), ((1, 2), (2, 3))),
        (((0, 3, 0, 4),), ((1, 5, 4), (0, 3))),
        (((1, 1, 5, 4),), ((1, 4), (0, 1, 5))),
    ),
    (6, 1, 2): (
        (((2, 1),), ((2, 1),)),
        (((2, 2),), ((2, 2),)),
        (((2, 3),), ((2, 3),)),
        (((2, 4),), ((0, 0, 4),)),
    ),
    (7, 0, 3): (
        (((1, 1), (2, 7)), ((2, 1), (0, 7))),
        (((0, 0), (2, 2)), ((0, 0), (1, 2))),
        (((0, 1), (1, 3)), ((0, 1), (1, 3))),
        (((2, 4), (0, 2)), ((1, 4), (2, 2))),
    ),
    (7, 0, 2): (
        (((2, 1),), ((2, 1),)),
        (((2, 2),), ((2, 2),)),
        (((2, 3),), ((2, 3),)),
        (((1, 1, 4),), ((0, 1, 4),)),
    ),
    (7, 1, 3): (
        (((2, 1), (0, 2, 7)), ((0, 1), (1, 2, 7))),
        (((0, 0), (1, 2)), ((0, 0), (2, 2))),
        (((1, 1), (2, 3)), ((1, 1), (0, 3))),
        (((1, 4), (2, 2)), ((1, 4), (0, 2))),
    ),
    (7, 1, 2): (
        (((2, 7),), ((2, 7),)),
        (((2, 0),), ((2, 0),)),
        (((2, 1),), ((2, 1),)),
        (((2, 2),), ((2, 2),)),
    ),
}


def place(x, y, core, z, half):
    return (x % XS * 8 + y % YS * 2 + core) * 16 + z % ZS * 2 + half


def everywhere():
    for x in range(XS):
        for y in range(YS):
            for core in range(2):
                for z in range(ZS):
                    for half in range(2):
                        yield x, y, core, z, half


def weight_plan():
    moves = {}
    found = {}
    for (z, half, kept), by_y in ROUTES.items():
        core = half if kept == 3 else 1 - half
        for x in range(XS):
            for y in range(YS):
                for part in range(PARTS):
                    for chain, *chips in by_y[y][part]:
                        at = place(x, y, core, z, half)
                        for step, chip in enumerate(chips):
                            to = place(x + chip // 4, chip % 4, core, z, half)
                            moves.setdefault((step, chain, part), []).append((at, to))
                            found[to, part, (x * 4 + y)] = (step, chain)
                            at = to
    order = sorted(moves)
    names = sorted({(step, chain) for step, chain, _ in order})
    table = np.zeros((256, PARTS, 3), np.int32)
    for x, y, core, z, half in everywhere():
        me = place(x, y, core, z, half)
        chip = 4 * x + y
        first = 2 if (half, core) == (1, 0) else 0
        second = 0 if (half, core) == (0, 1) else 2
        ends = (first, second) if core == 0 else (second, first)
        for part in range(PARTS):
            for slot, offset in enumerate((1,) + ends):
                source = (chip + z + offset) % 8
                if source != chip:
                    table[me, part, slot] = 1 + names.index(found[me, part, source])
    return {key: moves[key] for key in order}, names, table


def token_plan():
    shift = ([], [])
    flip = []
    near = ([], [])
    for x, y, core, z, half in everywhere():
        me = place(x, y, core, z, half)
        chip = 4 * x + y
        shift[core].append((me, place(x, y, half, z - chip - 1, half)))
        if core == half:
            flip.append((me, place(x, y, core, z, 1 - half)))
        first = 1 if (half, core) == (1, 0) else -1
        second = -1 if (half, core) == (0, 1) else 1
        near[0].append((place(x, y, core, z + first, half), me))
        near[1].append((place(x, y, core, z + second, half), me))
    return shift, flip, near


def product_kernel(slots, names, index, *refs):
    buffers = refs[: 1 + len(names) * PARTS]
    mid, end, out, held, sems = refs[1 + len(names) * PARTS :]
    rows = held.shape[2]

    def fetch(side, part, source):
        return pltpu.make_async_copy(source, held.at[side, part], sems.at[side, part])

    for part in range(PARTS):
        for side, slot in enumerate(slots):
            which = index[part * 3 + slot]

            @pl.when(which == 0)
            def _():
                fetch(side, part, buffers[0].at[pl.ds(part * rows, rows)]).start()

            for number in range(len(names)):

                @pl.when(which == 1 + number)
                def _():
                    fetch(side, part, buffers[1 + number * PARTS + part]).start()

    for part in range(PARTS):
        for side in range(2):
            fetch(side, part, buffers[0].at[pl.ds(part * rows, rows)]).wait()
    width = out.shape[1]
    for low in range(0, width, 256):
        high = min(low + 256, width)
        total = None
        for side, tokens in enumerate((mid, end)):
            for part in range(PARTS):
                term = jnp.dot(
                    tokens[:, part * rows : (part + 1) * rows],
                    held[side, part, :, low:high],
                    preferred_element_type=jnp.float32,
                )
                total = term if total is None else total + term
        out[:, low:high] = total


def product(slots, names, index, buffers, mid, end):
    count, (depth, width) = mid.shape[0], buffers[0].shape
    anywhere = pl.BlockSpec(memory_space=pl.ANY)
    whole = pl.BlockSpec(memory_space=pltpu.VMEM)
    return pl.pallas_call(
        functools.partial(product_kernel, slots, names),
        out_shape=jax.ShapeDtypeStruct((count, width), jnp.float32),
        in_specs=[pl.BlockSpec(memory_space=pltpu.SMEM)] + [anywhere] * len(buffers) + [whole] * 2,
        out_specs=whole,
        scratch_shapes=[
            pltpu.VMEM((2, PARTS, depth // PARTS, width), jnp.bfloat16),
            pltpu.SemaphoreType.DMA((2, PARTS)),
        ],
        compiler_params=pltpu.CompilerParams(vmem_limit_bytes=40 * 2**20),
        cost_estimate=pl.CostEstimate(
            flops=4 * count * depth * width, bytes_accessed=4 * depth * width + 4 * count * width, transcendentals=0
        ),
    )(index, *buffers, mid, end)


def on_device(tokens, gate_weight):
    me = lax.axis_index("row") * 16 + lax.axis_index("col")
    core = lax.axis_index("row") % 2
    half = lax.axis_index("col") % 2
    moves, names, table = weight_plan()
    index = lax.dynamic_index_in_dim(jnp.asarray(table.reshape(256, -1)), me, 0, keepdims=False)
    rows = gate_weight.shape[0] // PARTS
    parts = [gate_weight[part * rows : (part + 1) * rows] for part in range(PARTS)]

    shift, flip, near = token_plan()
    base = [lax.ppermute(tokens, BOTH, pairs) for pairs in shift]
    base = [jnp.where(core == half, own, lax.ppermute(own, BOTH, flip)) for own in base]
    ends = [lax.ppermute(own, BOTH, pairs) for own, pairs in zip(base, near)]

    got = {}
    for (step, chain, part), pairs in moves.items():
        source = parts[part] if step == 0 else got[step - 1, chain, part]
        got[step, chain, part] = lax.ppermute(source, BOTH, pairs)
    buffers = [gate_weight] + [got[name + (part,)] for name in names for part in range(PARTS)]

    keep_mid, send_mid = jnp.where(core == 0, base[0], base[1]), jnp.where(core == 0, base[1], base[0])
    keep_end, send_end = jnp.where(core == 0, ends[0], ends[1]), jnp.where(core == 0, ends[1], ends[0])
    send = product((0, 2), names, index, buffers, send_mid, send_end)
    swap = [(place(x, y, c, z, h), place(x, y, 1 - c, z, h)) for x, y, c, z, h in everywhere()]
    arrived = lax.ppermute(send, BOTH, swap)
    keep = product((0, 1), names, index, buffers, keep_mid, keep_end)
    return keep + arrived


def solution(mesh):
    placed = (P("row", "col"), P("row", "col"))
    return jax.shard_map(
        on_device, mesh=mesh, in_specs=placed, out_specs=P("row", "col"), check_vma=False
    )
```

```python
import functools

import jax
import jax.numpy as jnp
import numpy as np
from jax import lax
from jax.experimental import pallas as pl
from jax.experimental.pallas import tpu as pltpu
from jax.sharding import PartitionSpec as P

XS, YS, ZS = 2, 4, 8
BOTH = ("row", "col")
ROUNDS = 3
PARTS = 4

FIRST = (0,)
ROUTES = {
    (0, 0, 3): (
        (((0, 1, 7, 6),), ((0, 5, 6, 7),), ((0, 1, 6, 7),), ((0, 7, 6),)),
        (((0, 2, 0, 7),), ((0, 0, 7),), ((0, 2, 7, 0),), ((0, 2, 7, 0),)),
        (((0, 3, 1, 0),), ((0, 3, 0, 1),), ((0, 3, 0, 1),), ((0, 1, 0),)),
        (((0, 0, 2, 1),), ((0, 2, 1),), ((0, 0, 1, 2),), ((0, 0, 1, 2),)),
    ),
    (0, 0, 2): (
        (((0, 7),), ((0, 3, 7),), ((0, 3, 7),), ((0, 4, 7),)),
        (((0, 0),), ((0, 0),), ((0, 0),), ((0, 5, 0),)),
        (((0, 1),), ((0, 1),), ((0, 1),), ((0, 6, 1),)),
        (((0, 2),), ((0, 2),), ((0, 2),), ((0, 7, 2),)),
    ),
    (0, 1, 3): (
        (((0, 6, 7),), ((0, 6, 7),), ((0, 3, 7, 6),), ((0, 3, 7, 6),)),
        (((0, 7, 0),), ((0, 7, 0),), ((0, 0, 4, 7),), ((0, 0, 4, 7),)),
        (((0, 0, 1),), ((0, 0, 1),), ((0, 5, 1, 0),), ((0, 5, 1, 0),)),
        (((0, 1, 2),), ((0, 1, 2),), ((0, 2, 6, 1),), ((0, 2, 6, 1),)),
    ),
    (0, 1, 2): (
        (((0, 1, 6, 7),), ((0, 1, 6, 7),), ((0, 7, 6),), ((0, 7, 6),)),
        (((0, 0, 7),), ((0, 6, 7, 0),), ((0, 6, 7, 0),), ((0, 0, 7),)),
        (((0, 3, 0, 1),), ((0, 3, 0, 1),), ((0, 1, 0),), ((0, 1, 0),)),
        (((0, 2, 1),), ((0, 0, 1, 2),), ((0, 0, 1, 2),), ((0, 2, 1),)),
    ),
    (1, 0, 3): (
        (((0, 7, 6, 5),), ((0, 5, 6, 7),), ((0, 5, 6, 7),), ((0, 7, 6, 5),)),
        (((0, 0, 7, 6),), ((0, 6, 7, 0),), ((0, 6, 7, 0),), ((0, 6, 7, 0),)),
        (((0, 1, 0, 7),), ((0, 7, 0, 1),), ((0, 7, 0, 1),), ((0, 1, 0, 7),)),
        (((0, 2, 1, 0),), ((0, 0, 1, 2),), ((0, 0, 1, 2),), ((0, 0, 1, 2),)),
    ),
    (1, 0, 2): (
        (((0, 3, 7, 6),), ((0, 2, 6, 7),), ((0, 3, 7, 6),), ((0, 3, 7, 6),)),
        (((0, 0, 2, 7),), ((0, 5, 7, 0),), ((0, 0, 4, 7),), ((0, 0, 4, 7),)),
        (((0, 1, 0),), ((0, 3, 0, 1),), ((0, 5, 1, 0),), ((0, 1, 5, 0),)),
        (((0, 2, 1),), ((0, 0, 1, 2),), ((0, 2, 6, 1),), ((0, 2, 6, 1),)),
    ),
    (1, 1, 3): (
        (((0, 5, 6, 7),), ((0, 7, 6, 5),), ((0, 5, 6, 7),), ((0, 5, 6, 7),)),
        (((0, 0, 7, 6),), ((0, 0, 7, 6),), ((0, 6, 7, 0),), ((0, 0, 7, 6),)),
        (((0, 7, 0, 1),), ((0, 1, 0, 7),), ((0, 7, 0, 1),), ((0, 7, 0, 1),)),
        (((0, 2, 1, 0),), ((0, 2, 1, 0),), ((0, 0, 1, 2),), ((0, 2, 1, 0),)),
    ),
    (1, 1, 2): (
        (((0, 3, 6, 5),), ((0, 2, 5, 6),), ((0, 4, 5, 6),), ((0, 1, 6, 5),)),
        (((0, 6, 7),), ((0, 7, 6),), ((0, 7, 6),), ((0, 6, 7),)),
        (((0, 1, 0, 7),), ((0, 0, 3, 7),), ((0, 6, 7, 0),), ((0, 7, 0),)),
        (((0, 0, 1),), ((0, 1, 0),), ((0, 1, 0),), ((0, 0, 1),)),
    ),
    (2, 0, 3): (
        (((0, 4, 5, 6),), ((0, 4, 5, 6),), ((0, 4, 5, 6),), ((0, 4, 5, 6),)),
        (((0, 7, 6, 5),), ((0, 7, 6, 5),), ((0, 7, 6, 5),), ((0, 5, 6, 7),)),
        (((0, 6, 7, 0),), ((0, 6, 7, 0),), ((0, 6, 7, 0),), ((0, 6, 7, 0),)),
        (((0, 1, 0, 7),), ((0, 1, 0, 7),), ((0, 1, 0, 7),), ((0, 7, 0, 1),)),
    ),
    (2, 0, 2): (
        (((0, 5, 7, 6),), ((0, 2, 5, 6),), ((0, 1, 6, 5),), ((0, 1, 6, 5),)),
        (((0, 2, 6, 7),), ((0, 7, 6),), ((0, 6, 7),), ((0, 4, 7, 6),)),
        (((0, 7, 0),), ((0, 0, 7),), ((0, 7, 0),), ((0, 7, 0),)),
        (((0, 0, 1),), ((0, 1, 0),), ((0, 0, 1),), ((0, 2, 1, 0),)),
    ),
    (2, 1, 3): (
        (((0, 4, 5, 6),), ((0, 4, 5, 6),), ((0, 6, 5, 4),), ((0, 4, 5, 6),)),
        (((0, 7, 6, 5),), ((0, 5, 6, 7),), ((0, 7, 6, 5),), ((0, 7, 6, 5),)),
        (((0, 6, 7, 0),), ((0, 6, 7, 0),), ((0, 0, 7, 6),), ((0, 6, 7, 0),)),
        (((0, 1, 0, 7),), ((0, 7, 0, 1),), ((0, 1, 0, 7),), ((0, 1, 0, 7),)),
    ),
    (2, 1, 2): (
        (((0, 1, 4, 5),), ((0, 4, 5),), ((0, 3, 4, 5),), ((0, 1, 5, 4),)),
        (((0, 2, 5, 6),), ((0, 5, 6),), ((0, 6, 5),), ((0, 2, 6, 5),)),
        (((0, 7, 6),), ((0, 6, 7),), ((0, 1, 7, 6),), ((0, 4, 7, 6),)),
        (((0, 0, 7),), ((0, 7, 0),), ((0, 0, 2, 7),), ((0, 7, 0),)),
    ),
    (3, 0, 3): (
        (((0, 3, 4, 5),), ((0, 4, 5, 3),), ((0, 3, 4, 5),), ((0, 3, 4, 5),)),
        (((0, 6, 5, 4),), ((0, 5, 4, 6),), ((0, 4, 5, 6),), ((0, 6, 5, 4),)),
        (((0, 5, 6, 7),), ((0, 6, 7, 5),), ((0, 5, 6, 7),), ((0, 5, 6, 7),)),
        (((0, 0, 7, 6),), ((0, 7, 6, 0),), ((0, 6, 7, 0),), ((0, 0, 7, 6),)),
    ),
    (3, 0, 2): (
        (((0, 4, 5),), ((0, 5, 4),), ((0, 1, 5, 4),), ((0, 4, 5),)),
        (((0, 5, 6),), ((0, 6, 5),), ((0, 7, 6, 5),), ((0, 2, 6, 5),)),
        (((0, 6, 7),), ((0, 7, 6),), ((0, 6, 7),), ((0, 3, 7, 6),)),
        (((0, 7, 0),), ((0, 0, 7),), ((0, 0, 4, 7),), ((0, 1, 0, 7),)),
    ),
    (3, 1, 3): (
        (((0, 3, 4, 5),), ((0, 3, 4, 5),), ((0, 5, 4, 3),), ((0, 4, 5, 3),)),
        (((0, 6, 5, 4),), ((0, 6, 5, 4),), ((0, 6, 5, 4),), ((0, 5, 4, 6),)),
        (((0, 5, 6, 7),), ((0, 5, 6, 7),), ((0, 7, 6, 5),), ((0, 6, 7, 5),)),
        (((0, 0, 7, 6),), ((0, 0, 7, 6),), ((0, 0, 7, 6),), ((0, 7, 6, 0),)),
    ),
    (3, 1, 2): (
        (((0, 2, 3, 4),), ((0, 4, 3),), ((0, 3, 4),), ((0, 3, 7, 4),)),
        (((0, 0, 4, 5),), ((0, 5, 4),), ((0, 4, 5),), ((0, 5, 4),)),
        (((0, 1, 5, 6),), ((0, 6, 5),), ((0, 5, 6),), ((0, 4, 5, 6),)),
        (((0, 7, 6),), ((0, 7, 6),), ((0, 6, 7),), ((0, 2, 6, 7),)),
    ),
    (4, 0, 3): (
        (((0, 2, 3, 4),), ((0, 2, 3, 4),), ((0, 4, 3, 2),), ((0, 2, 3, 4),)),
        (((0, 5, 4, 3),), ((0, 3, 4, 5),), ((0, 5, 4, 3),), ((0, 5, 4, 3),)),
        (((0, 4, 5, 6),), ((0, 4, 5, 6),), ((0, 6, 5, 4),), ((0, 4, 5, 6),)),
        (((0, 7, 6, 5),), ((0, 5, 6, 7),), ((0, 7, 6, 5),), ((0, 7, 6, 5),)),
    ),
    (4, 0, 2): (
        (((0, 3, 1, 4),), ((0, 3, 4),), ((0, 4, 3),), ((0, 3, 7, 4),)),
        (((0, 0, 4, 5),), ((0, 4, 5),), ((0, 7, 4, 5),), ((0, 5, 4),)),
        (((0, 5, 6),), ((0, 1, 6, 5),), ((0, 1, 5, 6),), ((0, 6, 5),)),
        (((0, 2, 7, 6),), ((0, 2, 7, 6),), ((0, 2, 6, 7),), ((0, 0, 6, 7),)),
    ),
    (4, 1, 3): (
        (((0, 4, 3, 2),), ((0, 2, 3, 4),), ((0, 2, 3, 4),), ((0, 2, 3, 4),)),
        (((0, 5, 4, 3),), ((0, 5, 4, 3),), ((0, 5, 4, 3),), ((0, 5, 4, 3),)),
        (((0, 6, 5, 4),), ((0, 4, 5, 6),), ((0, 4, 5, 6),), ((0, 4, 5, 6),)),
        (((0, 7, 6, 5),), ((0, 7, 6, 5),), ((0, 7, 6, 5),), ((0, 7, 6, 5),)),
    ),
    (4, 1, 2): (
        (((0, 1, 2, 3),), ((0, 3, 2),), ((0, 2, 3),), ((0, 3, 2),)),
        (((0, 4, 3),), ((0, 4, 3),), ((0, 3, 4),), ((0, 4, 3),)),
        (((0, 7, 4, 5),), ((0, 1, 5, 4),), ((0, 4, 5),), ((0, 5, 4),)),
        (((0, 2, 5, 6),), ((0, 6, 4, 5),), ((0, 1, 6, 5),), ((0, 2, 5, 6),)),
    ),
    (5, 0, 3): (
        (((0, 1, 2, 3),), ((0, 1, 2, 3),), ((0, 3, 2, 1),), ((0, 1, 2, 3),)),
        (((0, 2, 3, 4),), ((0, 4, 3, 2),), ((0, 2, 3, 4),), ((0, 4, 3, 2),)),
        (((0, 3, 4, 5),), ((0, 3, 4, 5),), ((0, 5, 4, 3),), ((0, 3, 4, 5),)),
        (((0, 4, 5, 6),), ((0, 6, 5, 4),), ((0, 4, 5, 6),), ((0, 6, 5, 4),)),
    ),
    (5, 0, 2): (
        (((0, 3, 2),), ((0, 3, 2),), ((0, 2, 3),), ((0, 2, 3),)),
        (((0, 4, 3),), ((0, 4, 3),), ((0, 3, 0, 4),), ((0, 5, 4, 3),)),
        (((0, 5, 4),), ((0, 5, 4),), ((0, 4, 5),), ((0, 7, 5, 4),)),
        (((0, 2, 5, 6),), ((0, 6, 5),), ((0, 1, 6, 5),), ((0, 0, 6, 5),)),
    ),
    (5, 1, 3): (
        (((0, 1, 2, 3),), ((0, 3, 2, 1),), ((0, 3, 2, 1),), ((0, 3, 2, 1),)),
        (((0, 2, 3, 4),), ((0, 2, 3, 4),), ((0, 4, 3, 2),), ((0, 4, 3, 2),)),
        (((0, 3, 4, 5),), ((0, 5, 4, 3),), ((0, 5, 4, 3),), ((0, 5, 4, 3),)),
        (((0, 4, 5, 6),), ((0, 4, 5, 6),), ((0, 6, 5, 4),), ((0, 6, 5, 4),)),
    ),
    (5, 1, 2): (
        (((0, 1, 2),), ((0, 1, 5, 2),), ((0, 3, 2, 1),), ((0, 1, 5, 2),)),
        (((0, 2, 3),), ((0, 6, 2, 3),), ((0, 0, 3, 2),), ((0, 2, 6, 3),)),
        (((0, 3, 1, 4),), ((0, 3, 7, 4),), ((0, 6, 4, 3),), ((0, 3, 7, 4),)),
        (((0, 0, 4, 5),), ((0, 0, 4, 5),), ((0, 1, 5, 4),), ((0, 0, 4, 5),)),
    ),
    (6, 0, 3): (
        (((0, 1, 2),), ((0, 3, 2, 1),), ((0, 2, 1),), ((0, 2, 1),)),
        (((0, 2, 3),), ((0, 2, 3),), ((0, 3, 2),), ((0, 3, 2),)),
        (((0, 3, 4),), ((0, 1, 4, 3),), ((0, 4, 3),), ((0, 4, 3),)),
        (((0, 4, 5),), ((0, 4, 5),), ((0, 5, 4),), ((0, 5, 4),)),
    ),
    (6, 0, 2): (
        (((0, 3, 2, 1),), ((0, 1, 2),), ((0, 1, 5, 2),), ((0, 5, 1, 2),)),
        (((0, 0, 3, 2),), ((0, 0, 3, 2),), ((0, 6, 2, 3),), ((0, 2, 6, 3),)),
        (((0, 5, 4, 3),), ((0, 3, 4),), ((0, 3, 7, 4),), ((0, 3, 7, 4),)),
        (((0, 2, 5, 4),), ((0, 2, 5, 4),), ((0, 0, 4, 5),), ((0, 0, 4, 5),)),
    ),
    (6, 1, 3): (
        (((0, 3, 1, 2),), ((0, 3, 2, 1),), ((0, 1, 2),), ((0, 3, 2, 1),)),
        (((0, 0, 2, 3),), ((0, 0, 3, 2),), ((0, 0, 3, 2),), ((0, 2, 3),)),
        (((0, 1, 3, 4),), ((0, 5, 4, 3),), ((0, 3, 4),), ((0, 5, 4, 3),)),
        (((0, 6, 4, 5),), ((0, 2, 5, 4),), ((0, 2, 5, 4),), ((0, 4, 5),)),
    ),
    (6, 1, 2): (
        (((0, 1),), ((0, 1),), ((0, 1),), ((0, 4, 1),)),
        (((0, 2),), ((0, 2),), ((0, 2),), ((0, 5, 2),)),
        (((0, 3),), ((0, 3),), ((0, 3),), ((0, 6, 3),)),
        (((0, 0, 4),), ((0, 0, 4),), ((0, 4),), ((0, 7, 4),)),
    ),
    (7, 0, 3): (
        (((0, 7, 1),), ((0, 7, 1),), ((0, 7, 1),), ((0, 7, 1),)),
        (((0, 0, 2),), ((0, 0, 2),), ((0, 0, 2),), ((0, 0, 2),)),
        (((0, 1, 3),), ((0, 1, 3),), ((0, 1, 3),), ((0, 1, 3),)),
        (((0, 2, 4),), ((0, 2, 4),), ((0, 2, 4),), ((0, 2, 4),)),
    ),
    (7, 0, 2): (
        (((0, 1),), ((0, 1),), ((0, 1),), ((0, 1),)),
        (((0, 2),), ((0, 2),), ((0, 2),), ((0, 2),)),
        (((0, 3),), ((0, 3),), ((0, 3),), ((0, 3),)),
        (((0, 0, 4),), ((0, 0, 4),), ((0, 4),), ((0, 4),)),
    ),
    (7, 1, 3): (
        (((0, 1, 7),), ((0, 1, 7),), ((0, 1, 7),), ((0, 1, 7),)),
        (((0, 2, 0),), ((0, 2, 0),), ((0, 2, 0),), ((0, 2, 0),)),
        (((0, 3, 1),), ((0, 3, 1),), ((0, 3, 1),), ((0, 3, 1),)),
        (((0, 4, 2),), ((0, 4, 2),), ((0, 4, 2),), ((0, 4, 2),)),
    ),
    (7, 1, 2): (
        (((0, 3, 7),), ((0, 3, 7),), ((0, 7),), ((0, 7),)),
        (((0, 0),), ((0, 0),), ((0, 0),), ((0, 0),)),
        (((0, 1),), ((0, 1),), ((0, 1),), ((0, 1),)),
        (((0, 2),), ((0, 2),), ((0, 2),), ((0, 2),)),
    ),
}


def place(x, y, core, z, half):
    return (x % XS * 8 + y % YS * 2 + core) * 16 + z % ZS * 2 + half


def everywhere():
    for x in range(XS):
        for y in range(YS):
            for core in range(2):
                for z in range(ZS):
                    for half in range(2):
                        yield x, y, core, z, half


def weight_plan():
    moves = {}
    found = {}
    for (z, half, kept), by_y in ROUTES.items():
        core = half if kept == 3 else 1 - half
        for x in range(XS):
            for y in range(YS):
                for part in range(PARTS):
                    for chain, *chips in by_y[y][part]:
                        at = place(x, y, core, z, half)
                        for step, chip in enumerate(chips, FIRST[chain]):
                            to = place(x + chip // 4, chip % 4, core, z, half)
                            moves.setdefault((step, chain, part), []).append((at, to))
                            found[to, part, (x * 4 + y)] = (step, chain)
                            at = to
    keys = sorted(moves)
    table = np.zeros((256, PARTS, 3), np.int32)
    for x, y, core, z, half in everywhere():
        me = place(x, y, core, z, half)
        chip = 4 * x + y
        first = 2 if (half, core) == (1, 0) else 0
        second = 0 if (half, core) == (0, 1) else 2
        ends = (first, second) if core == 0 else (second, first)
        for part in range(PARTS):
            for slot, offset in enumerate((1,) + ends):
                source = (chip + z + offset) % 8
                if source != chip:
                    table[me, part, slot] = 1 + keys.index(found[me, part, source] + (part,))
    return {key: moves[key] for key in keys}, table


def token_plan():
    shift, first, second, keep, send = [], [], [], [], []
    for x, y, core, z, half in everywhere():
        me = place(x, y, core, z, half)
        shift.append((me, place(x, y, core, z - 4 * x - y - 1, half)))
        if core == half:
            first.append((me, place(x, y, core, z, 1 - half)))
        else:
            first.append((me, place(x, y, 1 - core, z, half)))
            second.append((me, place(x, y, 1 - core, z, 1 - half)))
        keep.append((place(x, y, core, z + (1 if half else -1), half), me))
        send.append((place(x, y, core, z + (-1 if core else 1), half), me))
    return shift, first, second, keep, send


def product_kernel(slots, last, rows, held_at, index, *refs):
    buffers = refs[: 1 + len(held_at)]
    tokens, out, held, sems = refs[1 + len(held_at) : -3 - last], refs[-3], refs[-2], refs[-1]
    jobs = [(part, side) for part in range(PARTS) for side in range(1 + last)]
    early = sum(step < ROUNDS - 1 for step, _, _ in held_at)

    def fetch(part, side, source):
        return pltpu.make_async_copy(source, held.at[side, part], sems.at[side, part])

    def own(part):
        return buffers[0].at[pl.ds(part * rows, rows)]

    def due(part, side):
        which = index[part * 3 + slots[side]]
        came_late = which > early
        if side:
            return which, which >= 0
        return which, came_late if last else jnp.logical_not(came_late)

    for part, side in jobs:
        which, wanted = due(part, side)
        if not last or side:

            @pl.when(which == 0)
            def _():
                fetch(part, side, own(part)).start()

        for number, (step, _, of) in enumerate(held_at, 1):
            if of == part and (side or last == (step == ROUNDS - 1)):

                @pl.when(which == number)
                def _():
                    fetch(part, side, buffers[number]).start()

    if not last:
        out[...] = jnp.zeros_like(out)
    width = out.shape[1]
    for part, side in jobs:

        @pl.when(due(part, side)[1])
        def _():
            fetch(part, side, own(part)).wait()
            for low in range(0, width, 256):
                high = min(low + 256, width)
                out[:, low:high] += jnp.dot(
                    tokens[side][:, part * rows : (part + 1) * rows],
                    held[side, part, :, low:high],
                    preferred_element_type=jnp.float32,
                )


def product(slots, index, own, got, mid, *more):
    last = bool(more)
    rows = own.shape[0] // PARTS
    held_at = sorted(key for key in got if last or key[0] < ROUNDS - 1)
    buffers = [own] + [got[key] for key in held_at]
    tokens, width = mid.shape[0], own.shape[1]
    anywhere = pl.BlockSpec(memory_space=pl.ANY)
    whole = pl.BlockSpec(memory_space=pltpu.VMEM)
    return pl.pallas_call(
        functools.partial(product_kernel, slots, last, rows, held_at),
        out_shape=jax.ShapeDtypeStruct((tokens, width), jnp.float32),
        in_specs=[pl.BlockSpec(memory_space=pltpu.SMEM)] + [anywhere] * len(buffers) + [whole] * (1 + len(more)),
        out_specs=whole,
        input_output_aliases={len(buffers) + 3: 0} if last else {},
        scratch_shapes=[
            pltpu.VMEM((1 + last, PARTS, rows, width), jnp.bfloat16),
            pltpu.SemaphoreType.DMA((1 + last, PARTS)),
        ],
        compiler_params=pltpu.CompilerParams(vmem_limit_bytes=40 * 2**20),
        cost_estimate=pl.CostEstimate(
            flops=2 * tokens * own.shape[0] * width,
            bytes_accessed=2 * own.shape[0] * width + 8 * tokens * width,
            transcendentals=0,
        ),
    )(index, *buffers, mid, *more)


def on_device(tokens, gate_weight):
    me = lax.axis_index("row") * 16 + lax.axis_index("col")
    core = lax.axis_index("row") % 2
    half = lax.axis_index("col") % 2
    moves, table = weight_plan()
    index = lax.dynamic_index_in_dim(jnp.asarray(table.reshape(256, -1)), me, 0, keepdims=False)
    rows = gate_weight.shape[0] // PARTS
    parts = [gate_weight[part * rows : (part + 1) * rows] for part in range(PARTS)]

    shift, first, second, near_keep, near_send = token_plan()

    def after(value, *others):
        return lax.optimization_barrier((value,) + others)[0]

    def send(value, pairs):
        return lax.ppermute(value, BOTH, pairs)

    got = {}

    def weights(step, part, *others):
        value = parts[part] if step == 0 else got[step - 1, 0, part]
        value = after(value, *others) if others else value
        got[step, 0, part] = send(value, moves[step, 0, part])
        return got[step, 0, part]

    def product_of(slots, *operands):
        return product(slots, index, gate_weight, *operands)

    shifted = send(tokens, shift)
    parts = [after(value, tokens) for value in parts]
    for part in range(PARTS):
        weights(0, part)
    weights(1, 0)
    weights(1, 1)
    weights(1, 2, shifted)
    shifted = after(shifted, got[0, 0, 0], got[0, 0, 1])
    crossed, also = send(shifted, first), send(shifted, second)
    weights(1, 3)
    weights(2, 0)
    weights(2, 1, crossed, also)
    keep_mid = jnp.where(core == half, shifted, crossed)
    send_mid = jnp.where(core == half, crossed, also)
    keep_end, send_end = send(keep_mid, near_keep), send(send_mid, near_send)
    weights(2, 2)
    weights(2, 3)
    early = {key: value for key, value in got.items() if key[0] < 2}
    sent = product_of((0, 2), early, send_mid)
    kept = product_of((0, 1), early, keep_mid)
    keep_end, send_end, sent, kept = lax.optimization_barrier((keep_end, send_end, sent, kept))
    sent = product_of((0, 2), got, send_mid, send_end, sent)
    swap = [(place(x, y, c, z, h), place(x, y, 1 - c, z, h)) for x, y, c, z, h in everywhere()]
    arrived = send(sent, swap)
    kept = product_of((0, 1), got, keep_mid, keep_end, kept)
    return kept + arrived

def solution(mesh):
    placed = (P("row", "col"), P("row", "col"))
    return jax.shard_map(
        on_device, mesh=mesh, in_specs=placed, out_specs=P("row", "col"), check_vma=False
    )
```

```python
import functools

import jax
import jax.numpy as jnp
import numpy as np
from jax import lax
from jax.experimental import pallas as pl
from jax.experimental.pallas import tpu as pltpu
from jax.sharding import PartitionSpec as P

XS, YS, ZS = 2, 4, 8
BOTH = ("row", "col")
ROUNDS = 4
PARTS = 4
WHEN = ((0, 1, 2), (0, 1, 3), (0, 2, 3), (1, 2, 3))

ROUTES = {
    (0, 0, 3): (
        ((1, 6, 7), (1, 6, 7), (6, 7), (7, 6)),
        ((2, 7, 0), (2, 7, 0), (5, 0, 7), (0, 7)),
        ((3, 0, 1), (3, 0, 1), (3, 1, 0), (1, 0)),
        ((0, 1, 2), (0, 1, 2), (0, 2, 1), (2, 1)),
    ),
    (0, 0, 2): (
        ((3, 7), (7,), (7,), (7,)),
        ((0,), (0,), (0,), (0,)),
        ((1,), (1,), (1,), (1,)),
        ((2,), (2,), (2,), (2,)),
    ),
    (0, 1, 3): (
        ((1, 6, 7), (1, 6, 7), (7, 6), (7, 6)),
        ((6, 7, 0), (7, 3, 0), (0, 3, 7), (0, 7)),
        ((3, 0, 1), (6, 0, 1), (1, 0), (1, 0)),
        ((0, 1, 2), (0, 1, 2), (2, 1), (2, 1)),
    ),
    (0, 1, 2): (
        ((1, 6, 7), (7, 6), (4, 7, 6), (7, 6)),
        ((2, 7, 0), (0, 7), (2, 0, 7), (0, 7)),
        ((3, 0, 1), (1, 0), (3, 1, 0), (1, 0)),
        ((0, 1, 2), (2, 1), (1, 2), (2, 1)),
    ),
    (1, 0, 3): (
        ((5, 6, 7), (7, 6, 5), (7, 6, 5), (7, 6, 5)),
        ((6, 7, 0), (6, 7, 0), (0, 7, 6), (6, 7, 0)),
        ((7, 0, 1), (1, 0, 7), (1, 0, 7), (1, 0, 7)),
        ((0, 1, 2), (0, 1, 2), (2, 1, 0), (0, 1, 2)),
    ),
    (1, 0, 2): (
        ((3, 6, 7), (1, 6, 7), (1, 6, 7), (7, 6)),
        ((2, 7, 0), (0, 7), (0, 7), (0, 3, 7)),
        ((1, 0), (3, 0, 1), (3, 0, 1), (1, 0)),
        ((0, 1, 2), (2, 1), (2, 1), (2, 1)),
    ),
    (1, 1, 3): (
        ((7, 6, 5), (5, 6, 7), (7, 6, 5), (5, 6, 7)),
        ((0, 7, 6), (0, 7, 6), (6, 7, 0), (0, 7, 6)),
        ((1, 0, 7), (7, 0, 1), (1, 0, 7), (7, 0, 1)),
        ((2, 1, 0), (2, 1, 0), (0, 1, 2), (2, 1, 0)),
    ),
    (1, 1, 2): (
        ((1, 6, 5), (2, 5, 6), (5, 6), (1, 6, 5)),
        ((6, 7), (7, 6), (6, 7), (6, 7)),
        ((7, 0), (0, 3, 7), (7, 0), (3, 0, 7)),
        ((0, 1), (1, 0), (0, 1), (0, 1)),
    ),
    (2, 0, 3): (
        ((6, 5, 4), (4, 5, 6), (4, 5, 6), (4, 5, 6)),
        ((7, 6, 5), (5, 6, 7), (5, 6, 7), (5, 6, 7)),
        ((0, 7, 6), (6, 7, 0), (6, 7, 0), (6, 7, 0)),
        ((1, 0, 7), (7, 0, 1), (7, 0, 1), (7, 0, 1)),
    ),
    (2, 0, 2): (
        ((3, 6, 5), (1, 6, 5), (1, 6, 5), (2, 6, 5)),
        ((0, 7, 6), (2, 7, 6), (2, 7, 6), (4, 7, 6)),
        ((1, 0, 7), (7, 4, 0), (3, 0, 7), (7, 5, 0)),
        ((2, 1, 0), (0, 1), (0, 1), (1, 0)),
    ),
    (2, 1, 3): (
        ((5, 4, 6), (4, 5, 6), (6, 5, 4), (4, 5, 6)),
        ((6, 7, 5), (5, 6, 7), (5, 6, 7), (7, 6, 5)),
        ((7, 6, 0), (6, 7, 0), (0, 7, 6), (6, 7, 0)),
        ((0, 1, 7), (7, 0, 1), (7, 0, 1), (1, 0, 7)),
    ),
    (2, 1, 2): (
        ((1, 4, 5), (4, 5), (1, 5, 4), (4, 5)),
        ((2, 5, 6), (5, 6), (2, 6, 5), (5, 6)),
        ((7, 6), (6, 7), (3, 7, 6), (6, 7)),
        ((0, 7), (7, 0), (0, 4, 7), (7, 4, 0)),
    ),
    (3, 0, 3): (
        ((4, 5, 3), (3, 4, 5), (5, 4, 3), (3, 4, 5)),
        ((5, 4, 6), (4, 5, 6), (4, 5, 6), (6, 5, 4)),
        ((6, 7, 5), (5, 6, 7), (7, 6, 5), (5, 6, 7)),
        ((7, 6, 0), (6, 7, 0), (6, 7, 0), (0, 7, 6)),
    ),
    (3, 0, 2): (
        ((4, 5), (5, 4), (1, 5, 4), (4, 5)),
        ((2, 6, 5), (6, 5), (2, 6, 5), (5, 6)),
        ((1, 7, 6), (7, 6), (3, 7, 6), (6, 7)),
        ((7, 0), (0, 7), (0, 4, 7), (7, 4, 0)),
    ),
    (3, 1, 3): (
        ((4, 5, 3), (5, 4, 3), (5, 4, 3), (3, 4, 5)),
        ((5, 4, 6), (6, 5, 4), (4, 5, 6), (6, 5, 4)),
        ((6, 7, 5), (7, 6, 5), (7, 6, 5), (5, 6, 7)),
        ((7, 6, 0), (0, 7, 6), (6, 7, 0), (0, 7, 6)),
    ),
    (3, 1, 2): (
        ((3, 7, 4), (3, 4), (3, 7, 4), (4, 7, 3)),
        ((0, 4, 5), (4, 5), (0, 4, 5), (5, 4)),
        ((1, 5, 6), (5, 6), (1, 5, 6), (6, 5)),
        ((2, 6, 7), (6, 7), (2, 6, 7), (7, 6)),
    ),
    (4, 0, 3): (
        ((3, 2, 4), (4, 3, 2), (4, 3, 2), (2, 3, 4)),
        ((4, 5, 3), (5, 4, 3), (3, 4, 5), (5, 4, 3)),
        ((6, 4, 5), (6, 5, 4), (6, 5, 4), (4, 5, 6)),
        ((5, 7, 6), (7, 6, 5), (5, 6, 7), (7, 6, 5)),
    ),
    (4, 0, 2): (
        ((3, 4), (4, 3), (3, 7, 4), (4, 7, 3)),
        ((4, 5), (5, 4), (0, 4, 5), (5, 4)),
        ((1, 6, 5), (6, 5), (1, 5, 6), (6, 5)),
        ((2, 7, 6), (7, 6), (2, 6, 7), (7, 6)),
    ),
    (4, 1, 3): (
        ((2, 3, 4), (4, 3, 2), (2, 3, 4), (4, 3, 2)),
        ((5, 4, 3), (3, 4, 5), (5, 4, 3), (5, 4, 3)),
        ((4, 5, 6), (6, 5, 4), (4, 5, 6), (6, 5, 4)),
        ((7, 6, 5), (5, 6, 7), (7, 6, 5), (7, 6, 5)),
    ),
    (4, 1, 2): (
        ((1, 2, 3), (3, 2), (3, 2), (2, 3)),
        ((2, 3, 4), (0, 3, 4), (4, 7, 3), (3, 0, 4)),
        ((3, 4, 5), (1, 4, 5), (1, 4, 5), (4, 5)),
        ((0, 5, 6), (2, 5, 6), (2, 5, 6), (1, 6, 5)),
    ),
    (5, 0, 3): (
        ((1, 2, 3), (1, 2, 3), (3, 2, 1), (1, 2, 3)),
        ((2, 3, 4), (4, 3, 2), (2, 3, 4), (4, 3, 2)),
        ((3, 4, 5), (3, 4, 5), (5, 4, 3), (3, 4, 5)),
        ((4, 5, 6), (6, 5, 4), (4, 5, 6), (6, 5, 4)),
    ),
    (5, 0, 2): (
        ((3, 2), (2, 3), (3, 2), (3, 2)),
        ((4, 3), (3, 0, 4), (4, 3), (0, 3, 4)),
        ((5, 4), (4, 5), (5, 4), (5, 4)),
        ((2, 5, 6), (1, 6, 5), (6, 5), (2, 5, 6)),
    ),
    (5, 1, 3): (
        ((3, 2, 1), (3, 2, 1), (1, 2, 3), (3, 2, 1)),
        ((4, 3, 2), (2, 3, 4), (2, 3, 4), (2, 3, 4)),
        ((5, 4, 3), (5, 4, 3), (3, 4, 5), (5, 4, 3)),
        ((6, 5, 4), (4, 5, 6), (4, 5, 6), (4, 5, 6)),
    ),
    (5, 1, 2): (
        ((3, 2, 1), (1, 2), (1, 2), (1, 2)),
        ((0, 3, 2), (2, 3), (0, 3, 2), (2, 3)),
        ((5, 4, 3), (3, 4), (3, 4), (3, 0, 4)),
        ((2, 5, 4), (0, 5, 4), (2, 5, 4), (4, 5)),
    ),
    (6, 0, 3): (
        ((3, 2, 1), (1, 2), (1, 2), (1, 2)),
        ((0, 3, 2), (2, 3), (2, 3), (2, 3)),
        ((5, 4, 3), (3, 4), (3, 4), (3, 0, 4)),
        ((2, 5, 4), (4, 5), (4, 5), (4, 5)),
    ),
    (6, 0, 2): (
        ((3, 2, 1), (3, 2, 1), (2, 1), (1, 2)),
        ((0, 3, 2), (5, 3, 2), (0, 2, 3), (2, 3)),
        ((1, 4, 3), (4, 0, 3), (1, 3, 4), (3, 4)),
        ((2, 5, 4), (2, 5, 4), (7, 4, 5), (4, 5)),
    ),
    (6, 1, 3): (
        ((3, 2, 1), (3, 2, 1), (3, 1, 2), (1, 2)),
        ((0, 3, 2), (0, 3, 2), (0, 2, 3), (2, 3)),
        ((1, 4, 3), (1, 4, 3), (6, 3, 4), (3, 4)),
        ((2, 5, 4), (2, 5, 4), (5, 4), (4, 5)),
    ),
    (6, 1, 2): (
        ((1,), (1,), (1,), (1,)),
        ((2,), (2,), (2,), (2,)),
        ((3,), (3,), (3,), (3,)),
        ((0, 4), (4,), (4,), (4,)),
    ),
    (7, 0, 3): (
        ((7, 3, 1), (7, 1), (7, 1), (7, 1)),
        ((4, 0, 2), (0, 2), (0, 2), (0, 2)),
        ((1, 5, 3), (1, 3), (1, 3), (1, 3)),
        ((2, 6, 4), (2, 4), (2, 4), (2, 4)),
    ),
    (7, 0, 2): (
        ((1,), (1,), (1,), (1,)),
        ((2,), (2,), (2,), (2,)),
        ((3,), (3,), (3,), (3,)),
        ((4,), (4,), (4,), (0, 4)),
    ),
    (7, 1, 3): (
        ((1, 5, 7), (1, 7), (1, 7), (1, 7)),
        ((6, 2, 0), (2, 0), (2, 0), (2, 0)),
        ((7, 3, 1), (3, 1), (3, 1), (3, 1)),
        ((4, 0, 2), (4, 2), (4, 2), (4, 2)),
    ),
    (7, 1, 2): (
        ((7,), (7,), (7,), (3, 7)),
        ((0,), (0,), (0,), (0,)),
        ((1,), (1,), (1,), (1,)),
        ((2,), (2,), (2,), (2,)),
    ),
}


def place(x, y, core, z, half):
    return (x % XS * 8 + y % YS * 2 + core) * 16 + z % ZS * 2 + half


def everywhere():
    for x in range(XS):
        for y in range(YS):
            for core in range(2):
                for z in range(ZS):
                    for half in range(2):
                        yield x, y, core, z, half


def weight_plan():
    moves = {}
    found = {}
    for (z, half, kept), by_y in ROUTES.items():
        core = half if kept == 3 else 1 - half
        for x in range(XS):
            for y in range(YS):
                for part in range(PARTS):
                    at = place(x, y, core, z, half)
                    for step, chip in zip(WHEN[part], by_y[y][part]):
                        to = place(x + chip // 4, chip % 4, core, z, half)
                        moves.setdefault((step, part), []).append((at, to))
                        found[to, part, x * 4 + y] = (step, part)
                        at = to
    keys = sorted(moves)
    table = np.zeros((256, PARTS, 3), np.int32)
    for x, y, core, z, half in everywhere():
        me = place(x, y, core, z, half)
        chip = 4 * x + y
        first = 2 if (half, core) == (1, 0) else 0
        second = 0 if (half, core) == (0, 1) else 2
        ends = (first, second) if core == 0 else (second, first)
        for part in range(PARTS):
            for slot, offset in enumerate((1,) + ends):
                source = (chip + z + offset) % 8
                if source != chip:
                    table[me, part, slot] = 1 + keys.index(found[me, part, source])
    return {key: moves[key] for key in keys}, table


def token_plan():
    start, shift, first, second, keep, send = [], [], [], [], [], []
    for x, y, core, z, half in everywhere():
        me = place(x, y, core, z, half)
        whole = (-4 * x - y - 1) % ZS
        whole -= ZS if whole > 4 or (whole == 4 and core) else 0
        some = {3: 2, 4: 2, 2: 1, 1: 1, 0: 0}[abs(whole)] * (1 if whole > 0 else -1)
        start.append((me, place(x, y, core, z + some, half)))
        shift.append((me, place(x, y, core, z + whole - some, half)))
        if core == half:
            first.append((me, place(x, y, core, z, 1 - half)))
        else:
            first.append((me, place(x, y, 1 - core, z, half)))
            second.append((me, place(x, y, 1 - core, z, 1 - half)))
        keep.append((place(x, y, core, z + (1 if half else -1), half), me))
        send.append((place(x, y, core, z + (-1 if core else 1), half), me))
    return start, shift, first, second, keep, send


def product_kernel(slots, last, rows, held_at, index, *refs):
    buffers = refs[: 1 + len(held_at)]
    tokens, out, held, sems = refs[1 + len(held_at) : -3 - last], refs[-3], refs[-2], refs[-1]
    jobs = [(part, side) for part in range(PARTS) for side in range(1 + last)]
    early = sum(step < ROUNDS - 1 for step, _ in held_at)

    def fetch(part, side, source):
        return pltpu.make_async_copy(source, held.at[side, part], sems.at[side, part])

    def own(part):
        return buffers[0].at[pl.ds(part * rows, rows)]

    def due(part, side):
        which = index[part * 3 + slots[side]]
        came_late = which > early
        if side:
            return which, which >= 0
        return which, came_late if last else jnp.logical_not(came_late)

    for part, side in jobs:
        which, wanted = due(part, side)
        if not last or side:

            @pl.when(which == 0)
            def _():
                fetch(part, side, own(part)).start()

        for number, (step, of) in enumerate(held_at, 1):
            if of == part and (side or last == (step == ROUNDS - 1)):

                @pl.when(which == number)
                def _():
                    fetch(part, side, buffers[number]).start()

    if not last:
        out[...] = jnp.zeros_like(out)
    width = out.shape[1]
    for part, side in jobs:

        @pl.when(due(part, side)[1])
        def _():
            fetch(part, side, own(part)).wait()
            for low in range(0, width, 256):
                high = min(low + 256, width)
                out[:, low:high] += jnp.dot(
                    tokens[side][:, part * rows : (part + 1) * rows],
                    held[side, part, :, low:high],
                    preferred_element_type=jnp.float32,
                )


def product(slots, index, own, got, mid, *more):
    last = bool(more)
    rows = own.shape[0] // PARTS
    held_at = sorted(key for key in got if last or key[0] < ROUNDS - 1)
    buffers = [own] + [got[key] for key in held_at]
    tokens, width = mid.shape[0], own.shape[1]
    anywhere = pl.BlockSpec(memory_space=pl.ANY)
    whole = pl.BlockSpec(memory_space=pltpu.VMEM)
    return pl.pallas_call(
        functools.partial(product_kernel, slots, last, rows, held_at),
        out_shape=jax.ShapeDtypeStruct((tokens, width), jnp.float32),
        in_specs=[pl.BlockSpec(memory_space=pltpu.SMEM)] + [anywhere] * len(buffers) + [whole] * (1 + len(more)),
        out_specs=whole,
        input_output_aliases={len(buffers) + 3: 0} if last else {},
        scratch_shapes=[
            pltpu.VMEM((1 + last, PARTS, rows, width), jnp.bfloat16),
            pltpu.SemaphoreType.DMA((1 + last, PARTS)),
        ],
        compiler_params=pltpu.CompilerParams(vmem_limit_bytes=40 * 2**20),
        cost_estimate=pl.CostEstimate(
            flops=2 * tokens * own.shape[0] * width,
            bytes_accessed=2 * own.shape[0] * width + 8 * tokens * width,
            transcendentals=0,
        ),
    )(index, *buffers, mid, *more)


def on_device(tokens, gate_weight):
    me = lax.axis_index("row") * 16 + lax.axis_index("col")
    core = lax.axis_index("row") % 2
    half = lax.axis_index("col") % 2
    moves, table = weight_plan()
    index = lax.dynamic_index_in_dim(jnp.asarray(table.reshape(256, -1)), me, 0, keepdims=False)
    rows = gate_weight.shape[0] // PARTS
    parts = [gate_weight[part * rows : (part + 1) * rows] for part in range(PARTS)]

    start, shift, first, second, near_keep, near_send = token_plan()

    def after(value, *others):
        return lax.optimization_barrier((value,) + others)[0]

    def send(value, pairs):
        return lax.ppermute(value, BOTH, pairs)

    got = {}

    def weights(step, part, *others):
        hop = WHEN[part].index(step)
        value = got[WHEN[part][hop - 1], part] if hop else parts[part]
        got[step, part] = send(after(value, *others) if others else value, moves[step, part])
        return got[step, part]

    def product_of(slots, *operands):
        return product(slots, index, gate_weight, *operands)

    shifted = send(tokens, start)
    parts = [after(value, tokens) for value in parts]
    a, b, c = weights(0, 0), weights(0, 1), weights(0, 2)
    a, b, c, shifted = weights(1, 0), weights(1, 1), weights(1, 3, c, shifted), send(after(shifted, a), shift)
    crossed, also = send(after(shifted, a), first), send(after(shifted, b), second)
    a, b, c = weights(2, 0), weights(2, 2, b), weights(2, 3, shifted)
    keep_mid = jnp.where(core == half, shifted, crossed)
    send_mid = jnp.where(core == half, crossed, also)
    keep_end, send_end = send(keep_mid, near_keep), send(send_mid, near_send)
    a, b, c = weights(3, 1, a, crossed, also), weights(3, 2), weights(3, 3)
    early = {key: value for key, value in got.items() if key[0] < ROUNDS - 1}
    sent = product_of((0, 2), early, send_mid)
    kept = product_of((0, 1), early, keep_mid)
    keep_end, send_end, sent, kept = lax.optimization_barrier((keep_end, send_end, sent, kept))
    sent = product_of((0, 2), got, send_mid, send_end, sent)
    swap = [(place(x, y, c, z, h), place(x, y, 1 - c, z, h)) for x, y, c, z, h in everywhere()]
    arrived = send(sent, swap)
    kept = product_of((0, 1), got, keep_mid, keep_end, kept)
    return kept + arrived

def solution(mesh):
    placed = (P("row", "col"), P("row", "col"))
    return jax.shard_map(
        on_device, mesh=mesh, in_specs=placed, out_specs=P("row", "col"), check_vma=False
    )
```

```python
import functools

import jax
import jax.numpy as jnp
import numpy as np
from jax import lax
from jax.experimental import pallas as pl
from jax.experimental.pallas import tpu as pltpu
from jax.sharding import PartitionSpec as P

XS, YS, ZS = 2, 4, 8
BOTH = ("row", "col")
ROUNDS = 4
SPARE = 0
PARTS = 4
WHEN = ((0, 1, 2), (0, 1, 3), (0, 2, 3), (1, 2, 3))

ROUTES = {
    (0, 0, 3): (
        ((1, 6, 7), (1, 6, 7), (6, 7), (7, 6)),
        ((2, 7, 0), (2, 7, 0), (5, 0, 7), (0, 7)),
        ((3, 0, 1), (3, 0, 1), (3, 1, 0), (1, 0)),
        ((0, 1, 2), (0, 1, 2), (0, 2, 1), (2, 1)),
    ),
    (0, 0, 2): (
        ((3, 7), (7,), (7,), (7,)),
        ((0,), (0,), (0,), (0,)),
        ((1,), (1,), (1,), (1,)),
        ((2,), (2,), (2,), (2,)),
    ),
    (0, 1, 3): (
        ((1, 6, 7), (1, 6, 7), (7, 6), (7, 6)),
        ((6, 7, 0), (7, 3, 0), (0, 3, 7), (0, 7)),
        ((3, 0, 1), (6, 0, 1), (1, 0), (1, 0)),
        ((0, 1, 2), (0, 1, 2), (2, 1), (2, 1)),
    ),
    (0, 1, 2): (
        ((1, 6, 7), (7, 6), (4, 7, 6), (7, 6)),
        ((2, 7, 0), (0, 7), (2, 0, 7), (0, 7)),
        ((3, 0, 1), (1, 0), (3, 1, 0), (1, 0)),
        ((0, 1, 2), (2, 1), (1, 2), (2, 1)),
    ),
    (1, 0, 3): (
        ((5, 6, 7), (5, 6, 7), (7, 6, 5), (7, 6, 5)),
        ((6, 7, 0), (6, 7, 0), (0, 7, 6), (6, 7, 0)),
        ((7, 0, 1), (7, 0, 1), (1, 0, 7), (1, 0, 7)),
        ((0, 1, 2), (0, 1, 2), (2, 1, 0), (0, 1, 2)),
    ),
    (1, 0, 2): (
        ((2, 6, 7), (7, 6), (3, 7, 6), (7, 6)),
        ((7, 3, 0), (0, 7), (0, 2, 7), (0, 7)),
        ((1, 0), (1, 0), (1, 0), (1, 0)),
        ((0, 1, 2), (2, 1), (2, 1), (2, 1)),
    ),
    (1, 1, 3): (
        ((7, 6, 5), (5, 6, 7), (7, 6, 5), (5, 6, 7)),
        ((0, 7, 6), (0, 7, 6), (6, 7, 0), (0, 7, 6)),
        ((1, 0, 7), (7, 0, 1), (1, 0, 7), (7, 0, 1)),
        ((2, 1, 0), (2, 1, 0), (0, 1, 2), (2, 1, 0)),
    ),
    (1, 1, 2): (
        ((1, 6, 5), (2, 5, 6), (5, 6), (1, 6, 5)),
        ((6, 7), (7, 6), (6, 7), (6, 7)),
        ((7, 0), (0, 3, 7), (7, 0), (3, 0, 7)),
        ((0, 1), (1, 0), (0, 1), (0, 1)),
    ),
    (2, 0, 3): (
        ((6, 5, 4), (4, 5, 6), (4, 5, 6), (4, 5, 6)),
        ((7, 6, 5), (5, 6, 7), (5, 6, 7), (5, 6, 7)),
        ((0, 7, 6), (6, 7, 0), (6, 7, 0), (6, 7, 0)),
        ((1, 0, 7), (7, 0, 1), (7, 0, 1), (7, 0, 1)),
    ),
    (2, 0, 2): (
        ((3, 6, 5), (1, 6, 5), (1, 6, 5), (2, 6, 5)),
        ((0, 7, 6), (2, 7, 6), (2, 7, 6), (4, 7, 6)),
        ((1, 0, 7), (7, 4, 0), (3, 0, 7), (7, 5, 0)),
        ((2, 1, 0), (0, 1), (0, 1), (1, 0)),
    ),
    (2, 1, 3): (
        ((4, 5, 6), (4, 5, 6), (6, 5, 4), (4, 5, 6)),
        ((6, 7, 5), (5, 6, 7), (5, 6, 7), (7, 6, 5)),
        ((7, 6, 0), (6, 7, 0), (0, 7, 6), (6, 7, 0)),
        ((1, 0, 7), (7, 0, 1), (7, 0, 1), (1, 0, 7)),
    ),
    (2, 1, 2): (
        ((1, 5, 4), (4, 5), (1, 5, 4), (4, 5)),
        ((2, 6, 5), (5, 6), (2, 6, 5), (5, 6)),
        ((3, 7, 6), (6, 7), (3, 7, 6), (6, 7)),
        ((0, 4, 7), (7, 4, 0), (0, 4, 7), (7, 0)),
    ),
    (3, 0, 3): (
        ((4, 5, 3), (3, 4, 5), (5, 4, 3), (3, 4, 5)),
        ((5, 4, 6), (4, 5, 6), (4, 5, 6), (6, 5, 4)),
        ((6, 7, 5), (5, 6, 7), (7, 6, 5), (5, 6, 7)),
        ((7, 6, 0), (6, 7, 0), (6, 7, 0), (0, 7, 6)),
    ),
    (3, 0, 2): (
        ((4, 5), (5, 4), (1, 5, 4), (4, 5)),
        ((2, 6, 5), (6, 5), (2, 6, 5), (5, 6)),
        ((1, 7, 6), (7, 6), (3, 7, 6), (6, 7)),
        ((7, 0), (0, 7), (0, 4, 7), (7, 4, 0)),
    ),
    (3, 1, 3): (
        ((4, 5, 3), (5, 4, 3), (5, 4, 3), (3, 4, 5)),
        ((5, 4, 6), (6, 5, 4), (4, 5, 6), (6, 5, 4)),
        ((6, 7, 5), (7, 6, 5), (7, 6, 5), (5, 6, 7)),
        ((7, 6, 0), (0, 7, 6), (6, 7, 0), (0, 7, 6)),
    ),
    (3, 1, 2): (
        ((3, 7, 4), (3, 4), (3, 7, 4), (4, 7, 3)),
        ((0, 4, 5), (4, 5), (0, 4, 5), (5, 4)),
        ((1, 5, 6), (5, 6), (1, 5, 6), (6, 5)),
        ((2, 6, 7), (6, 7), (2, 6, 7), (7, 6)),
    ),
    (4, 0, 3): (
        ((3, 2, 4), (4, 3, 2), (4, 3, 2), (2, 3, 4)),
        ((4, 5, 3), (5, 4, 3), (3, 4, 5), (5, 4, 3)),
        ((5, 4, 6), (6, 5, 4), (6, 5, 4), (4, 5, 6)),
        ((6, 7, 5), (7, 6, 5), (5, 6, 7), (7, 6, 5)),
    ),
    (4, 0, 2): (
        ((3, 4), (4, 3), (3, 7, 4), (4, 7, 3)),
        ((4, 5), (5, 4), (0, 4, 5), (5, 4)),
        ((1, 6, 5), (6, 5), (1, 5, 6), (6, 5)),
        ((2, 7, 6), (7, 6), (2, 6, 7), (7, 6)),
    ),
    (4, 1, 3): (
        ((2, 3, 4), (4, 3, 2), (2, 3, 4), (4, 3, 2)),
        ((5, 4, 3), (3, 4, 5), (5, 4, 3), (5, 4, 3)),
        ((4, 5, 6), (6, 5, 4), (4, 5, 6), (6, 5, 4)),
        ((7, 6, 5), (5, 6, 7), (7, 6, 5), (7, 6, 5)),
    ),
    (4, 1, 2): (
        ((1, 2, 3), (3, 2), (3, 2), (2, 3)),
        ((2, 3, 4), (0, 3, 4), (4, 7, 3), (3, 0, 4)),
        ((3, 4, 5), (1, 4, 5), (1, 4, 5), (4, 5)),
        ((0, 5, 6), (2, 5, 6), (2, 5, 6), (1, 6, 5)),
    ),
    (5, 0, 3): (
        ((1, 2, 3), (1, 2, 3), (3, 2, 1), (1, 2, 3)),
        ((2, 3, 4), (4, 3, 2), (2, 3, 4), (4, 3, 2)),
        ((3, 4, 5), (3, 4, 5), (5, 4, 3), (3, 4, 5)),
        ((4, 5, 6), (6, 5, 4), (4, 5, 6), (6, 5, 4)),
    ),
    (5, 0, 2): (
        ((3, 2), (2, 3), (3, 2), (3, 2)),
        ((4, 3), (3, 0, 4), (4, 3), (0, 3, 4)),
        ((5, 4), (4, 5), (5, 4), (5, 4)),
        ((2, 5, 6), (1, 6, 5), (6, 5), (2, 5, 6)),
    ),
    (5, 1, 3): (
        ((3, 2, 1), (3, 2, 1), (1, 2, 3), (3, 2, 1)),
        ((4, 3, 2), (4, 3, 2), (2, 3, 4), (2, 3, 4)),
        ((5, 4, 3), (5, 4, 3), (3, 4, 5), (5, 4, 3)),
        ((6, 5, 4), (6, 5, 4), (4, 5, 6), (4, 5, 6)),
    ),
    (5, 1, 2): (
        ((3, 2, 1), (1, 2), (1, 2), (1, 2)),
        ((2, 3), (2, 3), (2, 3), (2, 3)),
        ((4, 0, 3), (3, 4), (3, 1, 4), (3, 4)),
        ((1, 5, 4), (4, 5), (0, 4, 5), (4, 5)),
    ),
    (6, 0, 3): (
        ((3, 2, 1), (1, 2), (1, 2), (1, 2)),
        ((0, 3, 2), (2, 3), (2, 3), (2, 3)),
        ((5, 4, 3), (3, 4), (3, 4), (3, 0, 4)),
        ((2, 5, 4), (4, 5), (4, 5), (4, 5)),
    ),
    (6, 0, 2): (
        ((3, 2, 1), (3, 2, 1), (2, 1), (1, 2)),
        ((0, 3, 2), (5, 3, 2), (0, 2, 3), (2, 3)),
        ((1, 4, 3), (4, 0, 3), (1, 3, 4), (3, 4)),
        ((2, 5, 4), (2, 5, 4), (7, 4, 5), (4, 5)),
    ),
    (6, 1, 3): (
        ((3, 2, 1), (3, 2, 1), (3, 1, 2), (1, 2)),
        ((0, 3, 2), (0, 3, 2), (0, 2, 3), (2, 3)),
        ((1, 4, 3), (1, 4, 3), (6, 3, 4), (3, 4)),
        ((2, 5, 4), (2, 5, 4), (5, 4), (4, 5)),
    ),
    (6, 1, 2): (
        ((1,), (1,), (1,), (1,)),
        ((2,), (2,), (2,), (2,)),
        ((3,), (3,), (3,), (3,)),
        ((0, 4), (4,), (4,), (4,)),
    ),
    (7, 0, 3): (
        ((7, 3, 1), (7, 1), (7, 1), (7, 1)),
        ((4, 0, 2), (0, 2), (0, 2), (0, 2)),
        ((1, 5, 3), (1, 3), (1, 3), (1, 3)),
        ((2, 6, 4), (2, 4), (2, 4), (2, 4)),
    ),
    (7, 0, 2): (
        ((1,), (1,), (1,), (1,)),
        ((2,), (2,), (2,), (2,)),
        ((3,), (3,), (3,), (3,)),
        ((4,), (4,), (4,), (0, 4)),
    ),
    (7, 1, 3): (
        ((1, 5, 7), (1, 7), (1, 7), (1, 7)),
        ((6, 2, 0), (2, 0), (2, 0), (2, 0)),
        ((7, 3, 1), (3, 1), (3, 1), (3, 1)),
        ((4, 0, 2), (4, 2), (4, 2), (4, 2)),
    ),
    (7, 1, 2): (
        ((7,), (7,), (7,), (3, 7)),
        ((0,), (0,), (0,), (0,)),
        ((1,), (1,), (1,), (1,)),
        ((2,), (2,), (2,), (2,)),
    ),
}


def place(x, y, core, z, half):
    return (x % XS * 8 + y % YS * 2 + core) * 16 + z % ZS * 2 + half


def everywhere():
    for x in range(XS):
        for y in range(YS):
            for core in range(2):
                for z in range(ZS):
                    for half in range(2):
                        yield x, y, core, z, half


def weight_plan():
    moves = {}
    found = {}
    for (z, half, kept), by_y in ROUTES.items():
        core = half if kept == 3 else 1 - half
        for x in range(XS):
            for y in range(YS):
                for part in range(PARTS):
                    at = place(x, y, core, z, half)
                    for step, chip in zip(WHEN[part], by_y[y][part]):
                        to = place(x + chip // 4, chip % 4, core, z, half)
                        moves.setdefault((step, part), []).append((at, to))
                        found[to, part, x * 4 + y] = (step, part)
                        at = to
    keys = sorted(moves)
    table = np.zeros((256, PARTS, 3), np.int32)
    for x, y, core, z, half in everywhere():
        me = place(x, y, core, z, half)
        chip = 4 * x + y
        first = 2 if (half, core) == (1, 0) else 0
        second = 0 if (half, core) == (0, 1) else 2
        ends = (first, second) if core == 0 else (second, first)
        for part in range(PARTS):
            for slot, offset in enumerate((1,) + ends):
                source = (chip + z + offset) % 8
                if source != chip:
                    table[me, part, slot] = 1 + keys.index(found[me, part, source])
    return {key: moves[key] for key in keys}, table


def token_plan():
    start, shift, first, second, keep, send = [], [], [], [], [], []
    for x, y, core, z, half in everywhere():
        me = place(x, y, core, z, half)
        whole = (-4 * x - y - 1) % ZS
        whole -= ZS if whole > 4 or (whole == 4 and core) else 0
        some = {3: 2, 4: 2, 2: 1, 1: 1, 0: 0}[abs(whole)] * (1 if whole > 0 else -1)
        start.append((me, place(x, y, core, z + some, half)))
        shift.append((me, place(x, y, core, z + whole - some, half)))
        if core == half:
            first.append((me, place(x, y, core, z, 1 - half)))
        else:
            first.append((me, place(x, y, 1 - core, z, half)))
            second.append((me, place(x, y, 1 - core, z, 1 - half)))
        keep.append((place(x, y, core, z + (1 if half else -1), half), me))
        send.append((place(x, y, core, z + (-1 if core else 1), half), me))
    return start, shift, first, second, keep, send


def product_kernel(slots, last, rows, early, held_at, index, *refs):
    buffers, (mid, end) = refs[: 1 + len(held_at)], refs[1 + len(held_at) : 3 + len(held_at)]
    out, held, sems = refs[-3:]
    jobs = [(part, side) for part in range(PARTS) for side in range(2)]

    def fetch(part, side, source):
        return pltpu.make_async_copy(source, held.at[side, part], sems.at[side, part])

    def own(part):
        return buffers[0].at[pl.ds(part * rows, rows)]

    def due(part, side):
        which = index[part * 3 + slots[side]]
        return which, which > early if last else which <= early

    for part, side in jobs:
        which = due(part, side)[0]
        if not last:

            @pl.when(which == 0)
            def _():
                fetch(part, side, own(part)).start()

        for number, (_, of) in enumerate(held_at, 1 + early if last else 1):
            if of == part:

                @pl.when(which == number)
                def _():
                    fetch(part, side, buffers[number - early if last else number]).start()

    if not last:
        out[...] = jnp.zeros_like(out)
    width = out.shape[1]
    for part, side in jobs:

        @pl.when(due(part, side)[1])
        def _():
            fetch(part, side, own(part)).wait()
            for low in range(0, width, 256):
                high = min(low + 256, width)
                out[:, low:high] += jnp.dot(
                    (mid, end)[side][: out.shape[0], part * rows : (part + 1) * rows],
                    held[side, part, :, low:high],
                    preferred_element_type=jnp.float32,
                )


def product(slots, index, own, got, mid, end, *before):
    last = bool(before)
    rows = own.shape[0] // PARTS
    early = sum(key[0] < ROUNDS - 1 for key in got)
    held_at = sorted(key for key in got if last == (key[0] == ROUNDS - 1))
    buffers = [own] + [got[key] for key in held_at]
    count, width = mid.shape[0] - SPARE, own.shape[1]
    anywhere = pl.BlockSpec(memory_space=pl.ANY)
    whole = pl.BlockSpec(memory_space=pltpu.VMEM)
    return pl.pallas_call(
        functools.partial(product_kernel, slots, last, rows, early, held_at),
        out_shape=jax.ShapeDtypeStruct((count, width), jnp.float32),
        in_specs=[pl.BlockSpec(memory_space=pltpu.SMEM)] + [anywhere] * len(buffers) + [whole] * (2 + last),
        out_specs=whole,
        input_output_aliases={len(buffers) + 3: 0} if last else {},
        scratch_shapes=[
            pltpu.VMEM((2, PARTS, rows, width), jnp.bfloat16),
            pltpu.SemaphoreType.DMA((2, PARTS)),
        ],
        compiler_params=pltpu.CompilerParams(vmem_limit_bytes=24 * 2**20),
        cost_estimate=pl.CostEstimate(
            flops=2 * count * own.shape[0] * width,
            bytes_accessed=2 * own.shape[0] * width + 8 * count * width,
            transcendentals=0,
        ),
    )(index, *buffers, mid, end, *before)


def on_device(tokens, gate_weight):
    me = lax.axis_index("row") * 16 + lax.axis_index("col")
    core = lax.axis_index("row") % 2
    half = lax.axis_index("col") % 2
    moves, table = weight_plan()
    index = lax.dynamic_index_in_dim(jnp.asarray(table.reshape(256, -1)), me, 0, keepdims=False)
    rows = gate_weight.shape[0] // PARTS
    parts = [gate_weight[part * rows : (part + 1) * rows] for part in range(PARTS)]

    start, shift, first, second, near_keep, near_send = token_plan()

    def after(value, *others):
        return lax.optimization_barrier((value,) + others)[0]

    def send(value, pairs):
        return lax.ppermute(value, BOTH, pairs)

    got = {}

    def weights(step, part, *others):
        hop = WHEN[part].index(step)
        value = got[WHEN[part][hop - 1], part] if hop else parts[part]
        got[step, part] = send(after(value, *others) if others else value, moves[step, part])
        return got[step, part]

    def product_of(slots, *operands):
        return product(slots, index, gate_weight, got, *operands)

    shifted = send(tokens, start)
    parts = [after(value, tokens) for value in parts]
    a, b, c = weights(0, 0), weights(0, 1), weights(0, 2)
    a, b, c, shifted = weights(1, 0), weights(1, 1), weights(1, 3, c, shifted), send(after(shifted, a), shift)
    crossed, also = send(after(shifted, a), first), send(after(shifted, b), second)
    a, b, c = weights(2, 0), weights(2, 2, b), weights(2, 3, shifted)
    keep_mid = jnp.where(core == half, shifted, crossed)
    send_mid = jnp.where(core == half, crossed, also)
    keep_end, send_end = send(keep_mid, near_keep), send(send_mid, near_send)
    a, b, c = weights(3, 1, a, keep_mid, send_mid), weights(3, 2, keep_mid, send_mid), weights(3, 3, keep_mid, send_mid)
    sent = product_of((0, 2), send_mid, send_end)
    kept = product_of((0, 1), keep_mid, keep_end)
    got = dict(zip(got, lax.optimization_barrier((sent, kept) + tuple(got.values()))[2:]))
    sent = product_of((0, 2), send_mid, send_end, sent)
    swap = [(place(x, y, c, z, h), place(x, y, 1 - c, z, h)) for x, y, c, z, h in everywhere()]
    arrived = send(sent, swap)
    kept = product_of((0, 1), keep_mid, keep_end, kept)
    return kept + arrived

def solution(mesh):
    placed = (P("row", "col"), P("row", "col"))
    return jax.shard_map(
        on_device, mesh=mesh, in_specs=placed, out_specs=P("row", "col"), check_vma=False
    )
```

```python
import functools

import jax
import jax.numpy as jnp
import numpy as np
from jax import lax
from jax.experimental import pallas as pl
from jax.experimental.pallas import tpu as pltpu
from jax.sharding import PartitionSpec as P

XS, YS, ZS = 2, 4, 8
BOTH = ("row", "col")
ROUNDS = 4
SPARE = 0
PARTS = 4
WHEN = ((0, 1, 2), (0, 1, 3), (0, 2, 3), (1, 2, 3))

ROUTES = {
    (0, 0, 3): (
        ((1, 6, 7), (1, 6, 7), (6, 7), (7, 6)),
        ((2, 7, 0), (2, 7, 0), (5, 0, 7), (0, 7)),
        ((3, 0, 1), (3, 0, 1), (3, 1, 0), (1, 0)),
        ((0, 1, 2), (0, 1, 2), (0, 2, 1), (2, 1)),
    ),
    (0, 0, 2): (
        ((3, 7), (7,), (7,), (7,)),
        ((0,), (0,), (0,), (0,)),
        ((1,), (1,), (1,), (1,)),
        ((2,), (2,), (2,), (2,)),
    ),
    (0, 1, 3): (
        ((1, 6, 7), (1, 6, 7), (7, 6), (7, 6)),
        ((6, 7, 0), (7, 3, 0), (0, 3, 7), (0, 7)),
        ((3, 0, 1), (6, 0, 1), (1, 0), (1, 0)),
        ((0, 1, 2), (0, 1, 2), (2, 1), (2, 1)),
    ),
    (0, 1, 2): (
        ((1, 6, 7), (7, 6), (4, 7, 6), (7, 6)),
        ((2, 7, 0), (0, 7), (2, 0, 7), (0, 7)),
        ((3, 0, 1), (1, 0), (3, 1, 0), (1, 0)),
        ((0, 1, 2), (2, 1), (1, 2), (2, 1)),
    ),
    (1, 0, 3): (
        ((5, 6, 7), (5, 6, 7), (7, 6, 5), (7, 6, 5)),
        ((6, 7, 0), (6, 7, 0), (0, 7, 6), (6, 7, 0)),
        ((7, 0, 1), (7, 0, 1), (1, 0, 7), (1, 0, 7)),
        ((0, 1, 2), (0, 1, 2), (2, 1, 0), (0, 1, 2)),
    ),
    (1, 0, 2): (
        ((2, 6, 7), (7, 6), (3, 7, 6), (7, 6)),
        ((7, 3, 0), (0, 7), (0, 2, 7), (0, 7)),
        ((1, 0), (1, 0), (1, 0), (1, 0)),
        ((0, 1, 2), (2, 1), (2, 1), (2, 1)),
    ),
    (1, 1, 3): (
        ((7, 6, 5), (5, 6, 7), (7, 6, 5), (5, 6, 7)),
        ((0, 7, 6), (0, 7, 6), (6, 7, 0), (0, 7, 6)),
        ((1, 0, 7), (7, 0, 1), (1, 0, 7), (7, 0, 1)),
        ((2, 1, 0), (2, 1, 0), (0, 1, 2), (2, 1, 0)),
    ),
    (1, 1, 2): (
        ((1, 6, 5), (2, 5, 6), (5, 6), (1, 6, 5)),
        ((6, 7), (7, 6), (6, 7), (6, 7)),
        ((7, 0), (0, 3, 7), (7, 0), (3, 0, 7)),
        ((0, 1), (1, 0), (0, 1), (0, 1)),
    ),
    (2, 0, 3): (
        ((6, 5, 4), (4, 5, 6), (4, 5, 6), (4, 5, 6)),
        ((7, 6, 5), (5, 6, 7), (5, 6, 7), (5, 6, 7)),
        ((0, 7, 6), (6, 7, 0), (6, 7, 0), (6, 7, 0)),
        ((1, 0, 7), (7, 0, 1), (7, 0, 1), (7, 0, 1)),
    ),
    (2, 0, 2): (
        ((3, 6, 5), (1, 6, 5), (1, 6, 5), (2, 6, 5)),
        ((0, 7, 6), (2, 7, 6), (2, 7, 6), (4, 7, 6)),
        ((1, 0, 7), (7, 4, 0), (3, 0, 7), (7, 5, 0)),
        ((2, 1, 0), (0, 1), (0, 1), (1, 0)),
    ),
    (2, 1, 3): (
        ((4, 5, 6), (4, 5, 6), (6, 5, 4), (4, 5, 6)),
        ((6, 7, 5), (5, 6, 7), (5, 6, 7), (7, 6, 5)),
        ((7, 6, 0), (6, 7, 0), (0, 7, 6), (6, 7, 0)),
        ((1, 0, 7), (7, 0, 1), (7, 0, 1), (1, 0, 7)),
    ),
    (2, 1, 2): (
        ((1, 5, 4), (4, 5), (1, 5, 4), (4, 5)),
        ((2, 6, 5), (5, 6), (2, 6, 5), (5, 6)),
        ((3, 7, 6), (6, 7), (3, 7, 6), (6, 7)),
        ((0, 4, 7), (7, 4, 0), (0, 4, 7), (7, 0)),
    ),
    (3, 0, 3): (
        ((4, 5, 3), (3, 4, 5), (5, 4, 3), (3, 4, 5)),
        ((5, 4, 6), (4, 5, 6), (4, 5, 6), (6, 5, 4)),
        ((6, 7, 5), (5, 6, 7), (7, 6, 5), (5, 6, 7)),
        ((7, 6, 0), (6, 7, 0), (6, 7, 0), (0, 7, 6)),
    ),
    (3, 0, 2): (
        ((4, 5), (5, 4), (1, 5, 4), (4, 5)),
        ((2, 6, 5), (6, 5), (2, 6, 5), (5, 6)),
        ((1, 7, 6), (7, 6), (3, 7, 6), (6, 7)),
        ((7, 0), (0, 7), (0, 4, 7), (7, 4, 0)),
    ),
    (3, 1, 3): (
        ((4, 5, 3), (5, 4, 3), (5, 4, 3), (3, 4, 5)),
        ((5, 4, 6), (6, 5, 4), (4, 5, 6), (6, 5, 4)),
        ((6, 7, 5), (7, 6, 5), (7, 6, 5), (5, 6, 7)),
        ((7, 6, 0), (0, 7, 6), (6, 7, 0), (0, 7, 6)),
    ),
    (3, 1, 2): (
        ((3, 7, 4), (3, 4), (3, 7, 4), (4, 7, 3)),
        ((0, 4, 5), (4, 5), (0, 4, 5), (5, 4)),
        ((1, 5, 6), (5, 6), (1, 5, 6), (6, 5)),
        ((2, 6, 7), (6, 7), (2, 6, 7), (7, 6)),
    ),
    (4, 0, 3): (
        ((3, 2, 4), (4, 3, 2), (4, 3, 2), (2, 3, 4)),
        ((4, 5, 3), (5, 4, 3), (3, 4, 5), (5, 4, 3)),
        ((5, 4, 6), (6, 5, 4), (6, 5, 4), (4, 5, 6)),
        ((6, 7, 5), (7, 6, 5), (5, 6, 7), (7, 6, 5)),
    ),
    (4, 0, 2): (
        ((3, 4), (4, 3), (3, 7, 4), (4, 7, 3)),
        ((4, 5), (5, 4), (0, 4, 5), (5, 4)),
        ((1, 6, 5), (6, 5), (1, 5, 6), (6, 5)),
        ((2, 7, 6), (7, 6), (2, 6, 7), (7, 6)),
    ),
    (4, 1, 3): (
        ((2, 3, 4), (4, 3, 2), (2, 3, 4), (4, 3, 2)),
        ((5, 4, 3), (3, 4, 5), (5, 4, 3), (5, 4, 3)),
        ((4, 5, 6), (6, 5, 4), (4, 5, 6), (6, 5, 4)),
        ((7, 6, 5), (5, 6, 7), (7, 6, 5), (7, 6, 5)),
    ),
    (4, 1, 2): (
        ((1, 2, 3), (3, 2), (3, 2), (2, 3)),
        ((2, 3, 4), (0, 3, 4), (4, 7, 3), (3, 0, 4)),
        ((3, 4, 5), (1, 4, 5), (1, 4, 5), (4, 5)),
        ((0, 5, 6), (2, 5, 6), (2, 5, 6), (1, 6, 5)),
    ),
    (5, 0, 3): (
        ((1, 2, 3), (1, 2, 3), (3, 2, 1), (1, 2, 3)),
        ((2, 3, 4), (4, 3, 2), (2, 3, 4), (4, 3, 2)),
        ((3, 4, 5), (3, 4, 5), (5, 4, 3), (3, 4, 5)),
        ((4, 5, 6), (6, 5, 4), (4, 5, 6), (6, 5, 4)),
    ),
    (5, 0, 2): (
        ((3, 2), (2, 3), (3, 2), (3, 2)),
        ((4, 3), (3, 0, 4), (4, 3), (0, 3, 4)),
        ((5, 4), (4, 5), (5, 4), (5, 4)),
        ((2, 5, 6), (1, 6, 5), (6, 5), (2, 5, 6)),
    ),
    (5, 1, 3): (
        ((3, 2, 1), (3, 2, 1), (1, 2, 3), (3, 2, 1)),
        ((4, 3, 2), (4, 3, 2), (2, 3, 4), (2, 3, 4)),
        ((5, 4, 3), (5, 4, 3), (3, 4, 5), (5, 4, 3)),
        ((6, 5, 4), (6, 5, 4), (4, 5, 6), (4, 5, 6)),
    ),
    (5, 1, 2): (
        ((3, 2, 1), (1, 2), (1, 2), (1, 2)),
        ((2, 3), (2, 3), (2, 3), (2, 3)),
        ((4, 0, 3), (3, 4), (3, 1, 4), (3, 4)),
        ((1, 5, 4), (4, 5), (0, 4, 5), (4, 5)),
    ),
    (6, 0, 3): (
        ((3, 2, 1), (1, 2), (1, 2), (1, 2)),
        ((0, 3, 2), (2, 3), (2, 3), (2, 3)),
        ((5, 4, 3), (3, 4), (3, 4), (3, 0, 4)),
        ((2, 5, 4), (4, 5), (4, 5), (4, 5)),
    ),
    (6, 0, 2): (
        ((3, 2, 1), (3, 2, 1), (2, 1), (1, 2)),
        ((0, 3, 2), (5, 3, 2), (0, 2, 3), (2, 3)),
        ((1, 4, 3), (4, 0, 3), (1, 3, 4), (3, 4)),
        ((2, 5, 4), (2, 5, 4), (7, 4, 5), (4, 5)),
    ),
    (6, 1, 3): (
        ((3, 2, 1), (3, 2, 1), (3, 1, 2), (1, 2)),
        ((0, 3, 2), (0, 3, 2), (0, 2, 3), (2, 3)),
        ((1, 4, 3), (1, 4, 3), (6, 3, 4), (3, 4)),
        ((2, 5, 4), (2, 5, 4), (5, 4), (4, 5)),
    ),
    (6, 1, 2): (
        ((1,), (1,), (1,), (1,)),
        ((2,), (2,), (2,), (2,)),
        ((3,), (3,), (3,), (3,)),
        ((0, 4), (4,), (4,), (4,)),
    ),
    (7, 0, 3): (
        ((7, 3, 1), (7, 1), (7, 1), (7, 1)),
        ((4, 0, 2), (0, 2), (0, 2), (0, 2)),
        ((1, 5, 3), (1, 3), (1, 3), (1, 3)),
        ((2, 6, 4), (2, 4), (2, 4), (2, 4)),
    ),
    (7, 0, 2): (
        ((1,), (1,), (1,), (1,)),
        ((2,), (2,), (2,), (2,)),
        ((3,), (3,), (3,), (3,)),
        ((4,), (4,), (4,), (0, 4)),
    ),
    (7, 1, 3): (
        ((1, 5, 7), (1, 7), (1, 7), (1, 7)),
        ((6, 2, 0), (2, 0), (2, 0), (2, 0)),
        ((7, 3, 1), (3, 1), (3, 1), (3, 1)),
        ((4, 0, 2), (4, 2), (4, 2), (4, 2)),
    ),
    (7, 1, 2): (
        ((7,), (7,), (7,), (3, 7)),
        ((0,), (0,), (0,), (0,)),
        ((1,), (1,), (1,), (1,)),
        ((2,), (2,), (2,), (2,)),
    ),
}


def place(x, y, core, z, half):
    return (x % XS * 8 + y % YS * 2 + core) * 16 + z % ZS * 2 + half


def everywhere():
    for x in range(XS):
        for y in range(YS):
            for core in range(2):
                for z in range(ZS):
                    for half in range(2):
                        yield x, y, core, z, half


def weight_plan():
    moves = {}
    found = {}
    for (z, half, kept), by_y in ROUTES.items():
        core = half if kept == 3 else 1 - half
        for x in range(XS):
            for y in range(YS):
                for part in range(PARTS):
                    at = place(x, y, core, z, half)
                    for step, chip in zip(WHEN[part], by_y[y][part]):
                        to = place(x + chip // 4, chip % 4, core, z, half)
                        moves.setdefault((step, part), []).append((at, to))
                        found[to, part, x * 4 + y] = (step, part)
                        at = to
    keys = sorted(moves)
    table = np.zeros((256, PARTS, 3), np.int32)
    for x, y, core, z, half in everywhere():
        me = place(x, y, core, z, half)
        chip = 4 * x + y
        first = 2 if (half, core) == (1, 0) else 0
        second = 0 if (half, core) == (0, 1) else 2
        ends = (first, second) if core == 0 else (second, first)
        for part in range(PARTS):
            for slot, offset in enumerate((1,) + ends):
                source = (chip + z + offset) % 8
                if source != chip:
                    table[me, part, slot] = 1 + keys.index(found[me, part, source])
    return {key: moves[key] for key in keys}, table


def token_plan():
    start, shift, first, second, keep, send = [], [], [], [], [], []
    for x, y, core, z, half in everywhere():
        me = place(x, y, core, z, half)
        whole = (-4 * x - y - 1) % ZS
        whole -= ZS if whole > 4 or (whole == 4 and core) else 0
        some = {3: 2, 4: 2, 2: 1, 1: 1, 0: 0}[abs(whole)] * (1 if whole > 0 else -1)
        start.append((me, place(x, y, core, z + some, half)))
        shift.append((me, place(x, y, core, z + whole - some, half)))
        if core == half:
            first.append((me, place(x, y, core, z, 1 - half)))
        else:
            first.append((me, place(x, y, 1 - core, z, half)))
            second.append((me, place(x, y, 1 - core, z, 1 - half)))
        keep.append((place(x, y, core, z + (1 if half else -1), half), me))
        send.append((place(x, y, core, z + (-1 if core else 1), half), me))
    return start, shift, first, second, keep, send


def product_kernel(slots, last, rows, early, held_at, index, *refs):
    buffers, (mid, end) = refs[: 1 + len(held_at)], refs[1 + len(held_at) : 3 + len(held_at)]
    out, held, sems = refs[-3:]
    jobs = [(part, side) for part in range(PARTS) for side in range(2)]

    def fetch(part, side, source):
        return pltpu.make_async_copy(source, held.at[side, part], sems.at[side, part])

    def own(part):
        return buffers[0].at[pl.ds(part * rows, rows)]

    def due(part, side):
        which = index[part * 3 + slots[side]]
        return which, which > early if last else which <= early

    for part, side in jobs:
        which = due(part, side)[0]
        if not last:

            @pl.when(which == 0)
            def _():
                fetch(part, side, own(part)).start()

        for number, (_, of) in enumerate(held_at, 1 + early if last else 1):
            if of == part:

                @pl.when(which == number)
                def _():
                    fetch(part, side, buffers[number - early if last else number]).start()

    if not last:
        out[...] = jnp.zeros_like(out)
    width = out.shape[1]
    for part, side in jobs:

        @pl.when(due(part, side)[1])
        def _():
            fetch(part, side, own(part)).wait()
            for low in range(0, width, 256):
                high = min(low + 256, width)
                out[:, low:high] += jnp.dot(
                    (mid, end)[side][: out.shape[0], part * rows : (part + 1) * rows],
                    held[side, part, :, low:high],
                    preferred_element_type=jnp.float32,
                )


def product(slots, index, own, got, mid, end, *before):
    last = bool(before)
    rows = own.shape[0] // PARTS
    early = sum(key[0] < ROUNDS - 1 for key in got)
    held_at = sorted(key for key in got if last == (key[0] == ROUNDS - 1))
    buffers = [own] + [got[key] for key in held_at]
    count, width = mid.shape[0] - SPARE, own.shape[1]
    anywhere = pl.BlockSpec(memory_space=pl.ANY)
    whole = pl.BlockSpec(memory_space=pltpu.VMEM)
    return pl.pallas_call(
        functools.partial(product_kernel, slots, last, rows, early, held_at),
        out_shape=jax.ShapeDtypeStruct((count, width), jnp.float32),
        in_specs=[pl.BlockSpec(memory_space=pltpu.SMEM)] + [anywhere] * len(buffers) + [whole] * (2 + last),
        out_specs=whole,
        input_output_aliases={len(buffers) + 3: 0} if last else {},
        scratch_shapes=[
            pltpu.VMEM((2, PARTS, rows, width), jnp.bfloat16),
            pltpu.SemaphoreType.DMA((2, PARTS)),
        ],
        compiler_params=pltpu.CompilerParams(vmem_limit_bytes=16 * 2**20),
        cost_estimate=pl.CostEstimate(
            flops=2 * count * own.shape[0] * width,
            bytes_accessed=2 * own.shape[0] * width + 8 * count * width,
            transcendentals=0,
        ),
    )(index, *buffers, mid, end, *before)


def on_device(tokens, gate_weight):
    me = lax.axis_index("row") * 16 + lax.axis_index("col")
    core = lax.axis_index("row") % 2
    half = lax.axis_index("col") % 2
    moves, table = weight_plan()
    index = lax.dynamic_index_in_dim(jnp.asarray(table.reshape(256, -1)), me, 0, keepdims=False)
    rows = gate_weight.shape[0] // PARTS
    parts = [gate_weight[part * rows : (part + 1) * rows] for part in range(PARTS)]

    start, shift, first, second, near_keep, near_send = token_plan()

    def after(value, *others):
        return lax.optimization_barrier((value,) + others)[0]

    def send(value, pairs):
        return lax.ppermute(value, BOTH, pairs)

    got = {}

    def weights(step, part, *others):
        hop = WHEN[part].index(step)
        value = got[WHEN[part][hop - 1], part] if hop else parts[part]
        got[step, part] = send(after(value, *others) if others else value, moves[step, part])
        return got[step, part]

    def product_of(slots, *operands):
        return product(slots, index, gate_weight, got, *operands)

    shifted = send(tokens, start)
    parts = [after(value, tokens) for value in parts]
    a, b, c = weights(0, 0), weights(0, 1), weights(0, 2)
    a, b, c, shifted = weights(1, 0), weights(1, 1), weights(1, 3, c, shifted), send(after(shifted, a), shift)
    crossed, also = send(after(shifted, a), first), send(after(shifted, b), second)
    a, b, c = weights(2, 0), weights(2, 2, b), weights(2, 3, shifted)
    keep_mid = jnp.where(core == half, shifted, crossed)
    send_mid = jnp.where(core == half, crossed, also)
    keep_end, send_end = send(keep_mid, near_keep), send(send_mid, near_send)
    a, b, c = weights(3, 1, a, keep_mid, send_mid), weights(3, 2, keep_mid, send_mid), weights(3, 3, keep_mid, send_mid)
    sent = product_of((0, 2), send_mid, send_end)
    kept = product_of((0, 1), keep_mid, keep_end)
    got = dict(zip(got, lax.optimization_barrier((sent, kept) + tuple(got.values()))[2:]))
    sent = product_of((0, 2), send_mid, send_end, sent)
    swap = [(place(x, y, c, z, h), place(x, y, 1 - c, z, h)) for x, y, c, z, h in everywhere()]
    arrived = send(sent, swap)
    kept = product_of((0, 1), keep_mid, keep_end, kept)
    return kept + arrived

def solution(mesh):
    placed = (P("row", "col"), P("row", "col"))
    return jax.shard_map(
        on_device, mesh=mesh, in_specs=placed, out_specs=P("row", "col"), check_vma=False
    )
```
